32 devices in a mesh: chan: 4 (over y, x), patch: 8 (over z, core).
Axes of the slice: x: 2, y: 2, z: 4, core: 2. Of those that a mesh axis runs over, the one named last changes fastest.
Arguments:
- sky_maps: float32 [64, 24576], P('chan', 'patch')
- mode_vectors: float32 [64, 8], replicated
- pixel_weight: float32 [24576], P('patch'), may hold values from 0.3 to 3
- neighbours: int32 [12, 16, 9], P('chan', 'patch'), may hold values from 0 to 8, as said below
- tile_counts: int32 [12, 16], P('chan', 'patch'), may hold values from 0 to 9, as said below
- pair_bins: int32 [9, 128, 128], replicated, may hold values from 0 to 8, as said below
Outputs:
- correlation: float32 [4, 8, 8, 64, 64], P('chan', 'patch')
- covariance: float32 [64, 64], replicated
The draws below stay inside these ranges and needn't reach their ends.
Inputs may be any that keep to these rules, and one draw needn't show every extreme that they name: `neighbours`: for tile (A, B) the first tile_counts[A, B] entries are distinct offset codes o in ascending order, each naming the tile (A + o // 3 - 1, B + o % 3 - 1), which lies inside the grid and is observed; later entries mean nothing. An observed tile lists code 4 (itself); if a tile lists another, that one lists it back. `tile_counts`: 0 exactly for tiles that are not observed; some tile has 9. `pair_bins`: one table for each offset code, the same for every tile pair with that offset; the value 8 marks a pair beyond the last bin.
All inputs are finite; a program needn't handle non-finite values.
Results may differ from the reference program's by a relative error of at most 0.00075.
Values may be sent and summed in bfloat16 or wider, within the bound.
No kernel may reach another device: no remote copies, remote signals or barrier semaphores. Data moves between devices by JAX's collectives and lax.ppermute only.
A program may use at most 64 MiB of HBM per device.

```python
import math
import jax
import jax.numpy as jnp
from jax import lax

NCH = 64
MODES = 8
TILE = 128
NBIN = 8
NBR = 9
TA = 3
TB = 2
NTA = 12
NTB = 16
NPIX = 24576


def mode_table(key):
    return jax.random.normal(jax.random.fold_in(key, 11), (NCH, MODES), jnp.float32)


def draw_mode_vectors(key, part):
    return mode_table(key)


def draw_sky_maps(key, part):
    vectors = mode_table(key)
    key_list = [jax.random.fold_in(key, 20 + number) for number in range(6)]
    amplitude = 5.0 * jax.random.normal(key_list[0], (MODES, NTA * NTB * TILE), jnp.float32)
    foreground = jnp.dot(vectors, amplitude, precision=lax.Precision.HIGHEST, preferred_element_type=jnp.float32)
    gains = jnp.exp(jax.random.uniform(key_list[1], (NCH, 1, 1, 1), jnp.float32, math.log(0.5), math.log(5.0)))
    roughness = jax.random.normal(key_list[2], (NCH, NTA, NTB, TILE), jnp.float32)
    common = jax.random.normal(key_list[3], (1, NTA + 1, NTB + 1), jnp.float32)
    own_part = jax.random.normal(key_list[4], (NCH, NTA + 1, NTB + 1), jnp.float32)
    corner = common + own_part
    level = 0.25 * (corner[:, :-1, :-1] + corner[:, 1:, :-1] + corner[:, :-1, 1:] + corner[:, 1:, 1:])
    row_place = jnp.arange(NTA, dtype=jnp.float32)[:, None] / NTA
    col_place = jnp.arange(NTB, dtype=jnp.float32)[None, :] / NTB
    rising = jnp.exp(math.log(3.0) * (row_place + col_place))
    scatter = jnp.exp(jax.random.uniform(key_list[5], (1, NTA, NTB, TILE), jnp.float32, math.log(0.5), math.log(2.0)))
    signal = gains * rising[None, :, :, None] * (level[:, :, :, None] + 0.6 * roughness * scatter)
    total = foreground.reshape(NCH, NTA, NTB, TILE) + signal
    patch_count = NTB // TB
    total = total.reshape(NCH, NTA, patch_count, TB, TILE).transpose(0, 2, 1, 3, 4)
    return total.reshape(NCH, NTA * NTB * TILE)


def tile_graph(key):
    start_key = jax.random.fold_in(key, 31)
    toss_key = jax.random.fold_in(key, 32)
    drop_key = jax.random.fold_in(key, 33)
    hub_key = jax.random.fold_in(key, 34)
    band_rows = max(NTA // 4, 3)
    band_start = jax.random.randint(start_key, (), 0, NTA - band_rows + 1)
    row_index = jnp.arange(NTA, dtype=jnp.int32)[:, None]
    col_index = jnp.arange(NTB, dtype=jnp.int32)[None, :]
    coin_toss = jax.random.randint(toss_key, (NTA, NTB), 0, 100)
    in_band = (row_index >= band_start) & (row_index < band_start + band_rows)
    observed = (coin_toss < 35) | in_band
    padded = jnp.pad(observed, 1)
    keep_forward = jax.random.randint(drop_key, (NTA, NTB, 4), 0, 100) >= 20
    keep_padded = jnp.pad(keep_forward, ((1, 1), (1, 1), (0, 0)))
    hub_row = band_start + 1
    hub_col = jax.random.randint(hub_key, (), 1, NTB - 1)
    hub_tile = (row_index == hub_row) & (col_index == hub_col)
    hub_padded = jnp.pad(hub_tile, 1)
    live_list = []
    for offset_code in range(9):
        row_shift = offset_code // 3
        col_shift = offset_code % 3
        partner_seen = padded[row_shift:row_shift + NTA, col_shift:col_shift + NTB]
        if offset_code == 4:
            kept = jnp.ones((NTA, NTB), dtype=bool)
        elif offset_code > 4:
            kept = keep_forward[:, :, offset_code - 5]
        else:
            kept = keep_padded[row_shift:row_shift + NTA, col_shift:col_shift + NTB, 3 - offset_code]
        touches = hub_tile | hub_padded[row_shift:row_shift + NTA, col_shift:col_shift + NTB]
        live_list.append(observed & partner_seen & (kept | touches))
    live = jnp.stack(live_list, axis=-1).astype(jnp.int32)
    score = jnp.arange(9, dtype=jnp.int32)[None, None, :] + 9 * (1 - live)
    ordered = jnp.argsort(score, axis=-1, stable=True).astype(jnp.int32)
    counted = jnp.sum(live, axis=-1).astype(jnp.int32)
    return (ordered, counted)


def draw_neighbours(key, part):
    return tile_graph(key)[0]


def draw_tile_counts(key, part):
    return tile_graph(key)[1]


def draw_pair_bins(key, part):
    jitter_key = jax.random.fold_in(key, 41)
    codes = jnp.arange(NBR, dtype=jnp.int32)[:, None, None]
    first = jnp.arange(TILE, dtype=jnp.int32)[None, :, None]
    second = jnp.arange(TILE, dtype=jnp.int32)[None, None, :]
    row_gap = (codes // 3 - 1) * (TILE // 16) + second // 16 - first // 16
    col_gap = (codes % 3 - 1) * 16 + second % 16 - first % 16
    square = row_gap * row_gap + col_gap * col_gap
    geometric = jnp.zeros((NBR, TILE, TILE), jnp.int32)
    for level in range(1, NBIN + 1):
        geometric = geometric + (NBIN * NBIN * square >= 13 * level * (13 * level)).astype(jnp.int32)
    jitter = jax.random.randint(jitter_key, (NBR, TILE, TILE), -1, 2)
    jittered = jnp.clip(geometric + jitter, 0, NBIN - 1)
    return jnp.where(geometric < NBIN, jittered, NBIN).astype(jnp.int32)


def steps_of(key, extent, split, least, largest):
    gain, own = 1.0, jax.random.fold_in(key, 6)
    for dim, shards_of in split:
        steps = jnp.exp(jax.random.uniform(jax.random.fold_in(own, dim), (shards_of,), jnp.float32, least / len(split), largest / len(split)))
        gain = gain * jnp.repeat(steps, extent[dim] // shards_of).reshape([-1 if axis == dim else 1 for axis in range(len(extent))])
    return gain


def setup_inputs(seed: int = 0) -> dict:
    streams_of = jax.random.split(jax.random.key(seed), 7)
    return {
        "sky_maps": draw_sky_maps(jax.random.fold_in(streams_of[6], 71), 0),
        "mode_vectors": draw_mode_vectors(jax.random.fold_in(streams_of[6], 71), 0),
        "pixel_weight": jnp.clip(jnp.exp(math.log(3.0) - 2.3025851 * jax.random.uniform(streams_of[2], (NPIX,), jnp.float32) ** steps_of(streams_of[2], (NPIX,), ((0, 8),), -0.2, 0.2)), 0.3, 3.0),
        "neighbours": draw_neighbours(jax.random.fold_in(streams_of[6], 71), 0),
        "tile_counts": draw_tile_counts(jax.random.fold_in(streams_of[6], 71), 0),
        "pair_bins": draw_pair_bins(jax.random.fold_in(streams_of[6], 71), 0),
    }


def orthonormal_basis(mode_vectors):
    columns = []
    for number in range(MODES):
        vector = mode_vectors[:, number]
        for earlier in columns:
            vector = vector - jnp.sum(earlier * vector) * earlier
        columns.append(vector / jnp.sqrt(jnp.sum(vector * vector) + 1e-06))
    return jnp.stack(columns, axis=1)

def projector(mode_vectors):
    basis = orthonormal_basis(mode_vectors)
    outer = jnp.dot(basis, basis.T, precision=lax.Precision.HIGHEST, preferred_element_type=jnp.float32)
    return jnp.eye(NCH, dtype=jnp.float32) - outer

def bin_masks(pair_bins):
    levels = jnp.arange(NBIN, dtype=jnp.int32)
    table = pair_bins[:, :, None, :] == levels[None, None, :, None]
    return table.astype(jnp.bfloat16).reshape(NBR, TILE, NBIN * TILE)

def taper_table():
    return 0.75 + 0.25 * jnp.cos(math.pi * jnp.arange(NBIN, dtype=jnp.float32) / NBIN)

def reference(sky_maps, mode_vectors, pixel_weight, neighbours, tile_counts, pair_bins):
    patch_count = NTB // TB
    chan_count = NTA // TA
    project = projector(mode_vectors)
    cleaned = jnp.dot(project, sky_maps, precision=lax.Precision.HIGHEST, preferred_element_type=jnp.float32)
    weighted = (cleaned * pixel_weight[None, :]).astype(jnp.bfloat16)
    stacked = jnp.concatenate([weighted, pixel_weight.astype(jnp.bfloat16)[None, :]], axis=0)
    grid_tiles = stacked.reshape(NCH + 1, patch_count, NTA, TB, TILE).transpose(0, 2, 1, 3, 4)
    grid_tiles = grid_tiles.reshape(NCH + 1, NTA, NTB, TILE)
    observed = tile_counts > 0
    core_maps = grid_tiles[:NCH].astype(jnp.float32)
    masked = jnp.where(observed[None, :, :, None], core_maps, jnp.float32(0.0))
    pixel_total = jnp.sum(observed.astype(jnp.float32)) * TILE
    covariance = jnp.einsum('cabq,dabq->cd', masked, core_maps, precision=lax.Precision.HIGHEST) / pixel_total
    mask_table = bin_masks(pair_bins).astype(jnp.float32)
    padded = jnp.pad(grid_tiles, ((0, 0), (1, 1), (1, 1), (0, 0)))
    zero_index = jnp.zeros((), jnp.int32)

    def region_sums(region):
        region = jnp.asarray(region).astype(jnp.int32)
        chan_block = (region // patch_count).astype(jnp.int32)
        patch_block = (region % patch_count).astype(jnp.int32)

        def tile_step(position, running):
            position = jnp.asarray(position).astype(jnp.int32)
            row_at = (chan_block * TA + position // TB).astype(jnp.int32)
            col_at = (patch_block * TB + position % TB).astype(jnp.int32)
            centre = lax.dynamic_slice(padded, (zero_index, (row_at + 1).astype(jnp.int32), (col_at + 1).astype(jnp.int32), zero_index), (NCH + 1, 1, 1, TILE))
            centre = centre.reshape(NCH + 1, TILE).astype(jnp.float32)

            def slot_step(slot_number, carried):
                slot_number = jnp.asarray(slot_number).astype(jnp.int32)
                offset_code = neighbours[row_at, col_at, slot_number].astype(jnp.int32)
                row_partner = (row_at + offset_code // 3).astype(jnp.int32)
                col_partner = (col_at + offset_code % 3).astype(jnp.int32)
                partner = lax.dynamic_slice(padded, (zero_index, row_partner, col_partner, zero_index), (NCH + 1, 1, 1, TILE))
                partner = partner.reshape(NCH + 1, TILE).astype(jnp.float32)
                binned = jnp.dot(centre, mask_table[offset_code], precision=lax.Precision.HIGHEST, preferred_element_type=jnp.float32)
                binned = binned.astype(jnp.bfloat16).astype(jnp.float32).reshape(NCH + 1, NBIN, TILE)
                return carried + jnp.einsum('cbr,dr->bcd', binned, partner, precision=lax.Precision.HIGHEST)
            slot_limit = tile_counts[row_at, col_at].astype(jnp.int32)
            return lax.fori_loop(jnp.int32(0), slot_limit, slot_step, running)
        start_sums = jnp.zeros((NBIN, NCH + 1, NCH + 1), jnp.float32)
        return lax.fori_loop(jnp.int32(0), jnp.int32(TA * TB), tile_step, start_sums)
    pair_sums = lax.map(region_sums, jnp.arange(chan_count * patch_count, dtype=jnp.int32))
    spread = jnp.sqrt(jnp.diagonal(covariance) + 1e-06)
    norm_scale = spread[:, None] * spread[None, :]
    pair_weight = jnp.maximum(pair_sums[:, :, NCH, NCH], 1.0)
    correlation = taper_table()[None, :, None, None] * pair_sums[:, :, :NCH, :NCH]
    correlation = correlation / (pair_weight[:, :, None, None] * norm_scale[None, None])
    return (correlation.reshape(chan_count, patch_count, NBIN, NCH, NCH), covariance)
```

```python
import math

import jax
import jax.numpy as jnp
from jax import lax
from jax.experimental import pallas as pl
from jax.experimental.pallas import tpu as pltpu
from jax.sharding import PartitionSpec as P

NCH = 64
MODES = 8
TILE = 128
NBIN = 8
NBR = 9
TA = 3
TB = 2
EXT = TA + 2
WROW = EXT * NCH
COLH = WROW + 16
CHUNK = 512

F32 = jnp.float32
BF16 = jnp.bfloat16
ROWS_BY_ROWS = (((1,), (1,)), ((), ()))
VMEM = pl.BlockSpec(memory_space=pltpu.VMEM)
SMEM = pl.BlockSpec(memory_space=pltpu.SMEM)


def pieces(x):
    high = x.astype(BF16)
    rest = x - high.astype(F32)
    middle = rest.astype(BF16)
    low = (rest - middle.astype(F32)).astype(BF16)
    return high, middle, low


def projector_kernel(local_channels, modes_ref, project_ref):
    vectors = modes_ref[...].T
    lane = lax.broadcasted_iota(jnp.int32, (NCH, MODES), 1)
    for number in range(MODES):
        column = jnp.sum(jnp.where(lane == number, vectors, 0.0), axis=1, keepdims=True)
        inner = jnp.sum(column * vectors, axis=0, keepdims=True)
        square = jnp.sum(column * column, axis=0, keepdims=True)
        scale = 1.0 / jnp.sqrt(square + 1e-06)
        unit = column * scale
        reduced = vectors - unit * (inner * scale)
        vectors = jnp.where(lane == number, unit, jnp.where(lane > number, reduced, vectors))
    channel = lax.broadcasted_iota(jnp.int32, (NCH, NCH), 0)
    row = lax.broadcasted_iota(jnp.int32, (NCH, NCH), 1)
    holder = lax.axis_index("chan") ^ (row // local_channels)
    source = holder * local_channels + row % local_channels
    order = jnp.where(channel == source, 1.0, 0.0)
    ordered = lax.dot_general(
        order,
        vectors,
        (((0,), (0,)), ((), ())),
        precision=lax.Precision.HIGHEST,
        preferred_element_type=F32,
    )
    outer = lax.dot_general(
        vectors,
        ordered,
        ROWS_BY_ROWS,
        precision=lax.Precision.HIGHEST,
        preferred_element_type=F32,
    )
    high, middle, low = pieces(order - outer)
    none = jnp.zeros((NCH, NCH), BF16)
    project_ref[0:NCH, :] = jnp.concatenate([high, high, high], axis=1)
    project_ref[NCH : 2 * NCH, :] = jnp.concatenate([middle, middle, none], axis=1)
    project_ref[2 * NCH : 3 * NCH, :] = jnp.concatenate([low, none, none], axis=1)


def mask_kernel(bins_ref, mask_ref):
    for code in range(NBR):
        table = bins_ref[code]
        for level in range(NBIN):
            mask_ref[code, :, level * TILE : (level + 1) * TILE] = jnp.where(
                table == level, 1.0, 0.0
            ).astype(BF16)


def clean_kernel(block_count, *refs):
    counts_ref, project_ref, weight_ref = refs[:3]
    block_refs = refs[3 : 3 + block_count]
    cols_ref, near_ref, far_ref, cov_ref = refs[3 + block_count : 7 + block_count]
    padded_ref, masked_ref, weights_ref = refs[7 + block_count :]
    pixels = weight_ref.shape[1]
    row_pixels = TB * TILE
    region_pixels = TA * row_pixels
    chan_index = lax.axis_index("chan")
    side = lax.axis_index("patch") % 2

    for edge in (0, row_pixels + pixels):
        padded_ref[:, edge : edge + row_pixels] = jnp.zeros((NCH, row_pixels), BF16)
        weights_ref[:, edge : edge + row_pixels] = jnp.zeros((1, row_pixels), F32)
    weights_ref[:, row_pixels : row_pixels + pixels] = weight_ref[...]

    project = project_ref[...]
    observed_tiles = jnp.zeros((), jnp.int32)
    for begin in range(0, pixels, CHUNK):
        maps = jnp.concatenate([ref[:, begin : begin + CHUNK] for ref in block_refs], axis=0)
        split = jnp.concatenate(pieces(maps), axis=0)
        product = jnp.dot(project, split, preferred_element_type=F32)
        cleaned = (product[2 * NCH :] + product[NCH : 2 * NCH]) + product[:NCH]
        weighted = (cleaned * weight_ref[:, begin : begin + CHUNK]).astype(BF16)
        padded_ref[:, row_pixels + begin : row_pixels + begin + CHUNK] = weighted
        for place in range(begin, begin + CHUNK, TILE):
            tile = place // TILE
            holder = (tile // (TA * TB)) ^ chan_index
            observed = counts_ref[holder * (TA * TB) + tile % (TA * TB)] > 0
            observed_tiles = observed_tiles + observed.astype(jnp.int32)
            part = weighted[:, place - begin : place - begin + TILE]
            masked_ref[:, place : place + TILE] = jnp.where(observed, part, jnp.zeros_like(part))
    covariance = lax.dot_general(
        masked_ref[...],
        padded_ref[:, row_pixels : row_pixels + pixels],
        ROWS_BY_ROWS,
        preferred_element_type=F32,
    )
    total = jnp.full((NCH, NCH), (observed_tiles * TILE).astype(F32))
    cov_ref[...] = jnp.concatenate([covariance, total], axis=1)

    rows = lax.broadcasted_iota(jnp.int32, (16, TILE), 0)
    for col in range(TB):
        weight_rows = jnp.zeros((16, TILE), F32)
        for row in range(EXT):
            start = chan_index * region_pixels + row * row_pixels + col * TILE
            at = pl.ds(pl.multiple_of(start, TILE), TILE)
            cols_ref[col, row * NCH : (row + 1) * NCH, :] = padded_ref[:, at]
            weight_rows = jnp.where(rows == row, weights_ref[:, at], weight_rows)
        cols_ref[col, WROW:COLH, :] = weight_rows.astype(BF16)
    near_ref[...] = cols_ref[1 - side]
    far_ref[...] = cols_ref[side]


def add_pairs(code, live, centres, partners, mask_ref):
    row_shift = code // 3
    own = slice(NCH, (TA + 1) * NCH)
    left = jnp.concatenate(
        [column[own] for column in centres] + [column[WROW:] for column in centres], axis=0
    )
    binned = jnp.dot(left, mask_ref[code], preferred_element_type=F32).astype(BF16)
    rows = lax.broadcasted_iota(jnp.int32, (16, TILE), 0)
    right = []
    weight_sums = [jnp.zeros((16, TILE), F32) for _ in range(NBIN)]
    for col in range(TB):
        partner_weights = partners[col][WROW:].astype(F32)
        shifted = jnp.zeros((16, TILE), F32)
        for row in range(TA):
            present = live(row, col, code)
            place = row + row_shift
            tile = partners[col][place * NCH : (place + 1) * NCH]
            right.append(jnp.where(present, tile, jnp.zeros_like(tile)))
            weight = jnp.where(present, partner_weights[place : place + 1], 0.0)
            shifted = jnp.where(rows == row + 1, weight, shifted)
        first = TA * TB * NCH + col * 16
        for level in range(NBIN):
            lanes = slice(level * TILE, (level + 1) * TILE)
            weight_sums[level] += binned[first : first + 16, lanes].astype(F32) * shifted
    right = jnp.concatenate(right, axis=1)
    left = jnp.concatenate(
        [
            jnp.concatenate(
                [
                    binned[at * NCH : (at + 1) * NCH, level * TILE : (level + 1) * TILE]
                    for at in range(TA * TB)
                ],
                axis=1,
            )
            for level in range(NBIN)
        ],
        axis=0,
    )
    sums = lax.dot_general(left, right, ROWS_BY_ROWS, preferred_element_type=F32)
    return sums, weight_sums


def liveness(present_ref):
    return lambda row, col, code: present_ref[(row * TB + col) * NBR + code] > 0


def inner_kernel(present_ref, cols_ref, mask_ref, sums_ref, weight_sums_ref):
    live = liveness(present_ref)
    columns = [cols_ref[col] for col in range(TB)]
    for number, code in enumerate((1, 4, 7)):
        sums, weight_sums = add_pairs(code, live, columns, columns, mask_ref)
        if number:
            sums_ref[...] += sums
        else:
            sums_ref[...] = sums
        for level in range(NBIN):
            if number:
                weight_sums_ref[level] += weight_sums[level]
            else:
                weight_sums_ref[level] = weight_sums[level]


def outer_kernel(piece_count, *refs):
    present_ref, cols_ref, near_ref, far_ref, mask_ref, sums_in_ref, weight_in_ref = refs[:7]
    piece_refs = refs[7 : 7 + piece_count]
    corr_ref, cov_ref, sums_ref, weight_sums_ref = refs[7 + piece_count :]
    live = liveness(present_ref)
    even = lax.axis_index("patch") % 2 == 0
    columns = [cols_ref[col] for col in range(TB)]
    near, far = near_ref[...], far_ref[...]
    before = jnp.where(even, far, near)
    after = jnp.where(even, near, far)
    sums_ref[...] = sums_in_ref[...]
    weight_sums_ref[...] = weight_in_ref[...]
    for code in (0, 3, 6, 2, 5, 8):
        partners = [before, columns[0]] if code % 3 == 0 else [columns[1], after]
        sums, weight_sums = add_pairs(code, live, columns, partners, mask_ref)
        sums_ref[...] += sums
        for level in range(NBIN):
            weight_sums_ref[level] += weight_sums[level]

    whole = piece_refs[0][...]
    for ref in piece_refs[1:]:
        whole = whole + ref[...]
    covariance = whole[:, :NCH] / whole[:, NCH:]
    cov_ref[...] = covariance
    channel = lax.broadcasted_iota(jnp.int32, (NCH, NCH), 0)
    other = lax.broadcasted_iota(jnp.int32, (NCH, NCH), 1)
    diagonal = jnp.where(channel == other, covariance, 0.0)
    spread_down = jnp.sqrt(jnp.sum(diagonal, axis=1, keepdims=True) + 1e-06)
    spread_across = jnp.sqrt(jnp.sum(diagonal, axis=0, keepdims=True) + 1e-06)
    norm_scale = spread_down * spread_across
    for level in range(NBIN):
        taper = 0.75 + 0.25 * math.cos(math.pi * level / NBIN)
        total = jnp.sum(
            jnp.sum(weight_sums_ref[level], axis=1, keepdims=True), axis=0, keepdims=True
        )
        pair_weight = jnp.maximum(total, 1.0)
        sums = sums_ref[level * NCH : (level + 1) * NCH]
        corr_ref[level] = (taper * sums) / (pair_weight * norm_scale)


def run(kernel, outs, smem, args, scratch=()):
    return pl.pallas_call(
        kernel,
        out_shape=outs,
        in_specs=[SMEM] * smem + [VMEM] * (len(args) - smem),
        out_specs=jax.tree.map(lambda _: VMEM, outs),
        scratch_shapes=list(scratch),
        compiler_params=pltpu.CompilerParams(vmem_limit_bytes=24 * 2**20),
    )(*args)


def exchange(x, axis, step):
    count = lax.axis_size(axis)
    return lax.ppermute(x, axis, [(i, i ^ step) for i in range(count)])


def per_device(sky_maps, mode_vectors, pixel_weight, neighbours, tile_counts, pair_bins):
    shape = jax.ShapeDtypeStruct
    chan_count = lax.axis_size("chan")
    patch_count = lax.axis_size("patch")
    local_channels, pixels = sky_maps.shape

    blocks = [sky_maps] + [exchange(sky_maps, "chan", step) for step in range(1, chan_count)]
    counts = [tile_counts] + [exchange(tile_counts, "chan", step) for step in range(1, chan_count)]
    counts = jnp.concatenate([part.reshape(TA * TB) for part in counts])
    if local_channels % 16:
        blocks = [jnp.concatenate(blocks, axis=0)]

    project = run(
        lambda *refs: projector_kernel(local_channels, *refs),
        shape((3 * NCH, 3 * NCH), BF16),
        0,
        [mode_vectors.T],
    )
    mask = run(mask_kernel, shape((NBR, TILE, NBIN * TILE), BF16), 0, [pair_bins])
    codes = jnp.arange(NBR, dtype=jnp.int32)
    slot_live = codes[None, None, :] < tile_counts[:, :, None]
    matches = (neighbours[:, :, :, None] == codes) & slot_live[:, :, :, None]
    present = jnp.any(matches, axis=2).astype(jnp.int32).reshape(TA * TB * NBR)

    column = shape((COLH, TILE), BF16)
    cols, near, far, piece = run(
        lambda *refs: clean_kernel(len(blocks), *refs),
        (shape((TB, COLH, TILE), BF16), column, column, shape((NCH, 2 * NCH), F32)),
        1,
        [counts, project, pixel_weight.reshape(1, pixels)] + blocks,
        scratch=[
            pltpu.VMEM((NCH, pixels + 2 * TB * TILE), BF16),
            pltpu.VMEM((NCH, pixels), BF16),
            pltpu.VMEM((1, pixels + 2 * TB * TILE), F32),
        ],
    )

    near = exchange(near, "patch", 1)
    far_pairs = [(i, i + 1) for i in range(1, patch_count - 1, 2)]
    far = lax.ppermute(far, "patch", far_pairs + [(j, i) for i, j in far_pairs])

    piece = piece + exchange(piece, "patch", 1)
    stride = 2
    while True:
        group = min(4, patch_count // stride)
        parts = [piece] + [exchange(piece, "patch", stride * k) for k in range(1, group)]
        stride *= group
        if stride >= patch_count:
            break
        piece = sum(parts[1:], parts[0])

    sums_shape = shape((NBIN * NCH, NCH), F32)
    weight_shape = shape((NBIN, 16, TILE), F32)
    sums, weight_sums = run(inner_kernel, (sums_shape, weight_shape), 1, [present, cols, mask])
    correlation, covariance = run(
        lambda *refs: outer_kernel(len(parts), *refs),
        (shape((NBIN, NCH, NCH), F32), shape((NCH, NCH), F32)),
        1,
        [present, cols, near, far, mask, sums, weight_sums] + parts,
        scratch=[pltpu.VMEM((NBIN * NCH, NCH), F32), pltpu.VMEM((NBIN, 16, TILE), F32)],
    )
    return (correlation[None, None], covariance)


def solution(mesh):
    return jax.shard_map(
        per_device,
        mesh=mesh,
        in_specs=(
            P("chan", "patch"),
            P(),
            P("patch"),
            P("chan", "patch", None),
            P("chan", "patch"),
            P(),
        ),
        out_specs=(P("chan", "patch", None, None, None), P()),
        check_vma=False,
    )
```

```python
import math

import jax
import jax.numpy as jnp
from jax import lax
from jax.experimental import pallas as pl
from jax.experimental.pallas import tpu as pltpu
from jax.sharding import PartitionSpec as P

NCH = 64
MODES = 8
TILE = 128
NBIN = 8
NBR = 9
TA = 3
TB = 2
EXT = TA + 2
WROW = EXT * NCH
COLH = WROW + 16
CHUNK = 512

F32 = jnp.float32
BF16 = jnp.bfloat16
ROWS_BY_ROWS = (((1,), (1,)), ((), ()))
VMEM = pl.BlockSpec(memory_space=pltpu.VMEM)
SMEM = pl.BlockSpec(memory_space=pltpu.SMEM)
HBM = pl.BlockSpec(memory_space=pltpu.HBM)


def pieces(x):
    high = x.astype(BF16)
    rest = x - high.astype(F32)
    middle = rest.astype(BF16)
    low = (rest - middle.astype(F32)).astype(BF16)
    return high, middle, low


def prepare_kernel(counts_ref, maps_ref, joined_ref):
    local_channels, pixels = maps_ref.shape
    joined_ref[:, :pixels] = maps_ref[...]
    joined_ref[:, pixels:] = jnp.zeros((local_channels, joined_ref.shape[1] - pixels), F32)
    for tile in range(TA * TB):
        observed = jnp.where(counts_ref[tile % TB, tile // TB] > 0, 1.0, 0.0)
        row, lane = tile % local_channels, pixels + tile // local_channels * TILE
        joined_ref[row : row + 1, lane : lane + TILE] = jnp.full((1, TILE), observed)


def setting_kernel(
    local_channels,
    counts_ref,
    neighbours_ref,
    modes_ref,
    weight_ref,
    bins_ref,
    project_ref,
    padded_weight_ref,
    mask_ref,
    live_ref,
    held_counts,
    held_neighbours,
    held_modes,
    held_bins,
    copied,
):
    pixels = weight_ref.shape[1]
    edge = TB * TILE
    pairs = [
        (modes_ref, held_modes),
        (bins_ref, held_bins),
        (weight_ref, padded_weight_ref.at[:, pl.ds(edge, pixels)]),
        (counts_ref, held_counts),
        (neighbours_ref, held_neighbours),
    ]
    copies = [
        pltpu.make_async_copy(source, target, copied.at[number])
        for number, (source, target) in enumerate(pairs)
    ]
    for copy in copies:
        copy.start()
    padded_weight_ref[:, :edge] = jnp.zeros((1, edge), F32)
    padded_weight_ref[:, edge + pixels :] = jnp.zeros((1, edge), F32)
    copies[0].wait()
    vectors = held_modes[...].T
    lane = lax.broadcasted_iota(jnp.int32, (NCH, MODES), 1)
    for number in range(MODES):
        column = jnp.sum(jnp.where(lane == number, vectors, 0.0), axis=1, keepdims=True)
        inner = jnp.sum(column * vectors, axis=0, keepdims=True)
        square = jnp.sum(column * column, axis=0, keepdims=True)
        scale = 1.0 / jnp.sqrt(square + 1e-06)
        unit = column * scale
        reduced = vectors - unit * (inner * scale)
        vectors = jnp.where(lane == number, unit, jnp.where(lane > number, reduced, vectors))
    channel = lax.broadcasted_iota(jnp.int32, (NCH, NCH), 0)
    row = lax.broadcasted_iota(jnp.int32, (NCH, NCH), 1)
    holder = lax.axis_index("chan") ^ (row // local_channels)
    source = holder * local_channels + row % local_channels
    order = jnp.where(channel == source, 1.0, 0.0)
    ordered = lax.dot_general(
        order,
        vectors,
        (((0,), (0,)), ((), ())),
        precision=lax.Precision.HIGHEST,
        preferred_element_type=F32,
    )
    outer = lax.dot_general(
        vectors,
        ordered,
        ROWS_BY_ROWS,
        precision=lax.Precision.HIGHEST,
        preferred_element_type=F32,
    )
    high, middle, low = pieces(order - outer)
    none = jnp.zeros((NCH, NCH), BF16)
    project_ref[0:NCH, :] = jnp.concatenate([high, high, high], axis=1)
    project_ref[NCH : 2 * NCH, :] = jnp.concatenate([middle, middle, none], axis=1)
    project_ref[2 * NCH : 3 * NCH, :] = jnp.concatenate([low, none, none], axis=1)
    copies[1].wait()
    for code in range(NBR):
        table = held_bins[code]
        for level in range(NBIN):
            mask_ref[code, :, level * TILE : (level + 1) * TILE] = jnp.where(
                table == level, 1.0, 0.0
            ).astype(BF16)
    for copy in copies[2:]:
        copy.wait()
    for tile in range(TA * TB):
        count = held_counts[tile % TB, tile // TB]
        codes = jnp.zeros((), jnp.int32)
        for slot in range(NBR):
            code = held_neighbours[tile // TB, tile % TB, slot]
            codes = codes | jnp.where(slot < count, jnp.int32(1) << code, 0)
        for code in range(NBR):
            live = ((codes >> code) & 1).astype(F32)
            live_ref[code, tile] = jnp.full((16, TILE), live).astype(BF16)


def clean_kernel(block_count, flag_count, *refs):
    project_ref, weights_ref = refs[:2]
    block_refs = refs[2 : 2 + block_count]
    flag_refs = refs[2 + block_count : 2 + block_count + flag_count]
    cols_ref, near_ref, far_ref = refs[2 + block_count + flag_count :][:3]
    padded_ref, masked_ref, flags_ref = refs[5 + block_count + flag_count :]
    pixels = masked_ref.shape[1]
    row_pixels = TB * TILE
    region_pixels = TA * row_pixels
    region_tiles = TA * TB
    chan_index = lax.axis_index("chan")
    side = lax.axis_index("patch") % 2

    flags = [ref[...] for ref in flag_refs]
    flags += [ref[:8, pixels:] for ref in block_refs if ref.shape[1] > pixels]
    for step, rows in enumerate(flags):
        holder = chan_index ^ step
        flags_ref[pl.ds(pl.multiple_of(holder * 8, 8), 8), :] = rows
    for edge in (0, row_pixels + pixels):
        padded_ref[:, edge : edge + row_pixels] = jnp.zeros((NCH, row_pixels), BF16)

    project = project_ref[...]
    observed_tiles = jnp.zeros((1, TILE), F32)
    for begin in range(0, pixels, CHUNK):
        maps = jnp.concatenate([ref[:, begin : begin + CHUNK] for ref in block_refs], axis=0)
        split = jnp.concatenate(pieces(maps), axis=0)
        product = jnp.dot(project, split, preferred_element_type=F32)
        cleaned = (product[2 * NCH :] + product[NCH : 2 * NCH]) + product[:NCH]
        weights = weights_ref[:, row_pixels + begin : row_pixels + begin + CHUNK]
        weighted = cleaned * weights
        padded_ref[:, row_pixels + begin : row_pixels + begin + CHUNK] = weighted.astype(BF16)
        for place in range(begin, begin + CHUNK, TILE):
            tile = place // TILE
            at = tile // region_tiles * 8 + tile % region_tiles
            observed = flags_ref[at : at + 1, :]
            observed_tiles = observed_tiles + observed
            part = weighted[:, place - begin : place - begin + TILE]
            part = jnp.where(observed > 0, part, 0.0)
            masked_ref[:, place : place + TILE] = part.astype(BF16)
    covariance = lax.dot_general(
        masked_ref[...],
        padded_ref[:, row_pixels : row_pixels + pixels],
        ROWS_BY_ROWS,
        preferred_element_type=F32,
    )
    total = jnp.broadcast_to(observed_tiles[:, :NCH] * float(TILE), (NCH, NCH))
    near_ref[:NCH, :] = jnp.concatenate([covariance, total], axis=1)

    rows = lax.broadcasted_iota(jnp.int32, (16, TILE), 0)
    for col in range(TB):
        weight_rows = jnp.zeros((16, TILE), F32)
        for row in range(EXT):
            start = chan_index * region_pixels + row * row_pixels + col * TILE
            at = pl.ds(pl.multiple_of(start, TILE), TILE)
            cols_ref[col, row * NCH : (row + 1) * NCH, :] = padded_ref[:, at]
            weight_rows = jnp.where(rows == row, weights_ref[:, at], weight_rows)
        cols_ref[col, WROW:COLH, :] = weight_rows.astype(BF16)
    near_ref[NCH:, :] = cols_ref[1 - side].astype(F32)
    far_ref[...] = cols_ref[side]


def add_pairs(code, live_ref, centres, partners, mask_ref):
    row_shift = code // 3
    own = slice(NCH, (TA + 1) * NCH)
    left = jnp.concatenate(
        [column[own] for column in centres] + [column[WROW:] for column in centres], axis=0
    )
    binned = jnp.dot(left, mask_ref[code], preferred_element_type=F32).astype(BF16)
    rows = lax.broadcasted_iota(jnp.int32, (16, TILE), 0)
    right = []
    weight_sums = [jnp.zeros((16, TILE), F32) for _ in range(NBIN)]
    for col in range(TB):
        partner_weights = partners[col][WROW:].astype(F32)
        shifted = jnp.zeros((16, TILE), F32)
        for row in range(TA):
            live = live_ref[code, row * TB + col]
            place = row + row_shift
            tile = partners[col][place * NCH : (place + 1) * NCH]
            right.append(tile * jnp.concatenate([live] * (NCH // 16), axis=0))
            weight = partner_weights[place : place + 1] * live.astype(F32)[:1]
            shifted = jnp.where(rows == row + 1, weight, shifted)
        first = TA * TB * NCH + col * 16
        for level in range(NBIN):
            lanes = slice(level * TILE, (level + 1) * TILE)
            weight_sums[level] += binned[first : first + 16, lanes].astype(F32) * shifted
    right = jnp.concatenate(right, axis=1)
    left = jnp.concatenate(
        [
            jnp.concatenate(
                [
                    binned[at * NCH : (at + 1) * NCH, level * TILE : (level + 1) * TILE]
                    for at in range(TA * TB)
                ],
                axis=1,
            )
            for level in range(NBIN)
        ],
        axis=0,
    )
    sums = lax.dot_general(left, right, ROWS_BY_ROWS, preferred_element_type=F32)
    return sums, weight_sums


def inner_kernel(live_ref, cols_ref, mask_ref, sums_ref, weight_sums_ref, none_ref):
    none_ref[...] = jnp.zeros_like(none_ref)
    columns = [cols_ref[col] for col in range(TB)]
    for number, code in enumerate((1, 4, 7)):
        sums, weight_sums = add_pairs(code, live_ref, columns, columns, mask_ref)
        if number:
            sums_ref[...] += sums
        else:
            sums_ref[...] = sums
        for level in range(NBIN):
            if number:
                weight_sums_ref[level] += weight_sums[level]
            else:
                weight_sums_ref[level] = weight_sums[level]


def outer_kernel(
    live_ref,
    cols_ref,
    near_ref,
    far_ref,
    mask_ref,
    sums_in_ref,
    weight_in_ref,
    sums_ref,
    weight_sums_ref,
):
    even = lax.axis_index("patch") % 2 == 0
    columns = [cols_ref[col] for col in range(TB)]
    near, far = near_ref[NCH:].astype(BF16), far_ref[...]
    before = jnp.where(even, far, near)
    after = jnp.where(even, near, far)
    sums_ref[...] = sums_in_ref[...]
    weight_sums_ref[...] = weight_in_ref[...]
    for code in (0, 3, 6, 2, 5, 8):
        partners = [before, columns[0]] if code % 3 == 0 else [columns[1], after]
        sums, weight_sums = add_pairs(code, live_ref, columns, partners, mask_ref)
        sums_ref[...] += sums
        for level in range(NBIN):
            weight_sums_ref[level] += weight_sums[level]


def scale_kernel(sums_ref, weight_sums_ref, piece_ref, other_piece_ref, corr_ref, cov_ref):
    whole = piece_ref[...] + other_piece_ref[...]
    covariance = whole[:, :NCH] / whole[:, NCH:]
    cov_ref[...] = covariance
    channel = lax.broadcasted_iota(jnp.int32, (NCH, NCH), 0)
    other = lax.broadcasted_iota(jnp.int32, (NCH, NCH), 1)
    diagonal = jnp.where(channel == other, covariance, 0.0)
    spread_down = jnp.sqrt(jnp.sum(diagonal, axis=1, keepdims=True) + 1e-06)
    spread_across = jnp.sqrt(jnp.sum(diagonal, axis=0, keepdims=True) + 1e-06)
    norm_scale = spread_down * spread_across
    for level in range(NBIN):
        taper = 0.75 + 0.25 * math.cos(math.pi * level / NBIN)
        total = jnp.sum(
            jnp.sum(weight_sums_ref[level], axis=1, keepdims=True), axis=0, keepdims=True
        )
        pair_weight = jnp.maximum(total, 1.0)
        sums = sums_ref[level * NCH : (level + 1) * NCH]
        corr_ref[level] = (taper * sums) / (pair_weight * norm_scale)


def run(kernel, outs, args, scratch=(), spec=VMEM):
    return pl.pallas_call(
        kernel,
        out_shape=outs,
        in_specs=[spec] * len(args),
        out_specs=jax.tree.map(lambda _: VMEM, outs),
        scratch_shapes=list(scratch),
        compiler_params=pltpu.CompilerParams(vmem_limit_bytes=24 * 2**20),
    )(*args)


def exchange(x, axis, step):
    count = lax.axis_size(axis)
    return lax.ppermute(x, axis, [(i, i ^ step) for i in range(count)])


def per_device(sky_maps, mode_vectors, pixel_weight, neighbours, tile_counts, pair_bins):
    shape = jax.ShapeDtypeStruct
    chan_count = lax.axis_size("chan")
    patch_count = lax.axis_size("patch")
    local_channels, pixels = sky_maps.shape

    counts = tile_counts.T
    flag_lanes = -(-TA * TB // local_channels) * TILE
    joined = pl.pallas_call(
        prepare_kernel,
        out_shape=shape((local_channels, pixels + flag_lanes), F32),
        in_specs=[SMEM, VMEM],
        out_specs=VMEM,
        compiler_params=pltpu.CompilerParams(vmem_limit_bytes=24 * 2**20),
    )(counts, sky_maps)
    blocks = [joined] + [exchange(joined, "chan", step) for step in range(1, chan_count)]
    all_flags = []
    if local_channels % 16:
        for block in blocks:
            rows = [
                block[t % local_channels, pixels + t // local_channels * TILE :][:TILE]
                for t in range(TA * TB)
            ]
            all_flags.append(jnp.pad(jnp.stack(rows), ((0, 8 - TA * TB), (0, 0))))
        blocks = [jnp.concatenate([block[:, :pixels] for block in blocks], axis=0)]
    project, weights, mask, live = run(
        lambda *refs: setting_kernel(local_channels, *refs),
        (
            shape((3 * NCH, 3 * NCH), BF16),
            shape((1, pixels + 2 * TB * TILE), F32),
            shape((NBR, TILE, NBIN * TILE), BF16),
            shape((NBR, TA * TB, 16, TILE), BF16),
        ),
        [counts, neighbours, mode_vectors.T, pixel_weight.reshape(1, pixels), pair_bins],
        scratch=[
            pltpu.SMEM((TB, TA), jnp.int32),
            pltpu.SMEM((TA, TB, NBR), jnp.int32),
            pltpu.VMEM((MODES, NCH), F32),
            pltpu.VMEM((NBR, TILE, TILE), jnp.int32),
            pltpu.SemaphoreType.DMA((5,)),
        ],
        spec=HBM,
    )

    cols, near, far = run(
        lambda *refs: clean_kernel(len(blocks), len(all_flags), *refs),
        (shape((TB, COLH, TILE), BF16), shape((NCH + COLH, TILE), F32), shape((COLH, TILE), BF16)),
        [project, weights] + blocks + all_flags,
        scratch=[
            pltpu.VMEM((NCH, pixels + 2 * TB * TILE), BF16),
            pltpu.VMEM((NCH, pixels), BF16),
            pltpu.VMEM((chan_count * 8, TILE), F32),
        ],
    )

    received = exchange(near, "patch", 1)
    far_pairs = [(i, i + 1) for i in range(1, patch_count - 1, 2)]
    far = lax.ppermute(far, "patch", far_pairs + [(j, i) for i, j in far_pairs])
    piece = near[:NCH] + received[:NCH]
    other_piece = exchange(piece, "patch", 2)
    sums_shape = shape((NBIN * NCH, NCH), F32)
    weight_shape = shape((NBIN, 16, TILE), F32)
    pair_shapes = (sums_shape, weight_shape)
    none_shape = shape((NCH, 2 * NCH), F32)
    sums, weight_sums, none = run(inner_kernel, pair_shapes + (none_shape,), [live, cols, mask])
    step = 4
    while step < patch_count:
        piece = piece + other_piece + none
        other_piece = exchange(piece, "patch", step)
        step *= 2

    sums, weight_sums = run(
        outer_kernel, pair_shapes, [live, cols, received, far, mask, sums, weight_sums]
    )
    correlation, covariance = run(
        scale_kernel,
        (shape((NBIN, NCH, NCH), F32), shape((NCH, NCH), F32)),
        [sums, weight_sums, piece, other_piece],
    )
    return (correlation[None, None], covariance)


def solution(mesh):
    return jax.shard_map(
        per_device,
        mesh=mesh,
        in_specs=(
            P("chan", "patch"),
            P(),
            P("patch"),
            P("chan", "patch", None),
            P("chan", "patch"),
            P(),
        ),
        out_specs=(P("chan", "patch", None, None, None), P()),
        check_vma=False,
    )
```

```python
import math

import jax
import jax.numpy as jnp
from jax import lax
from jax.experimental import pallas as pl
from jax.experimental.pallas import tpu as pltpu
from jax.sharding import PartitionSpec as P

NCH = 64
MODES = 8
TILE = 128
NBIN = 8
NBR = 9
TA = 3
TB = 2
EXT = TA + 2
WROW = EXT * NCH
COLH = WROW + 16
ROW = TB * TILE
REGION = TA * ROW

F32 = jnp.float32
BF16 = jnp.bfloat16
ROWS_BY_ROWS = (((1,), (1,)), ((), ()))
VMEM = pl.BlockSpec(memory_space=pltpu.VMEM)
HBM = pl.BlockSpec(memory_space=pltpu.HBM)


def pieces(x):
    high = x.astype(BF16)
    rest = x - high.astype(F32)
    middle = rest.astype(BF16)
    low = (rest - middle.astype(F32)).astype(BF16)
    return high, middle, low


def prepare_kernel(maps_ref, *refs):
    *block_refs, held, copied = refs
    chan_index = lax.axis_index("chan")
    last = len(block_refs) - 1
    pixels = maps_ref.shape[1]
    copy = pltpu.make_async_copy(maps_ref, held, copied)
    copy.start()
    copy.wait()
    for step, ref in enumerate(block_refs):
        holder = chan_index ^ step
        start = pl.multiple_of(holder * REGION, ROW)
        above = pl.multiple_of(jnp.maximum(start - ROW, 0), ROW)
        below = pl.multiple_of(jnp.minimum(start + REGION, pixels - ROW), ROW)
        ref[:, :ROW] = jnp.where(holder > 0, held[:, pl.ds(above, ROW)], 0.0)
        ref[:, ROW : ROW + REGION] = held[:, pl.ds(start, REGION)]
        ref[:, ROW + REGION :] = jnp.where(holder < last, held[:, pl.ds(below, ROW)], 0.0)


def setting_kernel(
    local_channels,
    counts_ref,
    neighbours_ref,
    modes_ref,
    weight_ref,
    bins_ref,
    project_ref,
    padded_weight_ref,
    mask_ref,
    live_ref,
    held_counts,
    held_neighbours,
    held_modes,
    held_bins,
    copied,
):
    pixels = weight_ref.shape[1]
    edge = ROW
    pairs = [
        (modes_ref, held_modes),
        (bins_ref, held_bins),
        (weight_ref, padded_weight_ref.at[:, pl.ds(edge, pixels)]),
        (counts_ref, held_counts),
        (neighbours_ref, held_neighbours),
    ]
    copies = [
        pltpu.make_async_copy(source, target, copied.at[number])
        for number, (source, target) in enumerate(pairs)
    ]
    for copy in copies:
        copy.start()
    padded_weight_ref[:, :edge] = jnp.zeros((1, edge), F32)
    padded_weight_ref[:, edge + pixels :] = jnp.zeros((1, edge), F32)
    copies[0].wait()
    vectors = held_modes[...].T
    lane = lax.broadcasted_iota(jnp.int32, (NCH, MODES), 1)
    for number in range(MODES):
        column = jnp.sum(jnp.where(lane == number, vectors, 0.0), axis=1, keepdims=True)
        inner = jnp.sum(column * vectors, axis=0, keepdims=True)
        square = jnp.sum(column * column, axis=0, keepdims=True)
        scale = 1.0 / jnp.sqrt(square + 1e-06)
        unit = column * scale
        reduced = vectors - unit * (inner * scale)
        vectors = jnp.where(lane == number, unit, jnp.where(lane > number, reduced, vectors))
    channel = lax.broadcasted_iota(jnp.int32, (NCH, NCH), 0)
    row = lax.broadcasted_iota(jnp.int32, (NCH, NCH), 1)
    holder = lax.axis_index("chan") ^ (row // local_channels)
    source = holder * local_channels + row % local_channels
    order = jnp.where(channel == source, 1.0, 0.0)
    ordered = lax.dot_general(
        order,
        vectors,
        (((0,), (0,)), ((), ())),
        precision=lax.Precision.HIGHEST,
        preferred_element_type=F32,
    )
    outer = lax.dot_general(
        vectors,
        ordered,
        ROWS_BY_ROWS,
        precision=lax.Precision.HIGHEST,
        preferred_element_type=F32,
    )
    high, middle, low = pieces(order - outer)
    none = jnp.zeros((NCH, NCH), BF16)
    project_ref[0:NCH, :] = jnp.concatenate([high, high, high], axis=1)
    project_ref[NCH : 2 * NCH, :] = jnp.concatenate([middle, middle, none], axis=1)
    project_ref[2 * NCH : 3 * NCH, :] = jnp.concatenate([low, none, none], axis=1)
    copies[1].wait()
    for code in range(NBR):
        table = held_bins[code]
        for level in range(NBIN):
            mask_ref[code, :, level * TILE : (level + 1) * TILE] = jnp.where(
                table == level, 1.0, 0.0
            ).astype(BF16)
    for copy in copies[2:]:
        copy.wait()
    for tile in range(TA * TB):
        count = held_counts[tile % TB, tile // TB]
        codes = jnp.zeros((), jnp.int32)
        for slot in range(NBR):
            code = held_neighbours[tile // TB, tile % TB, slot]
            codes = codes | jnp.where(slot < count, jnp.int32(1) << code, 0)
        for code in range(NBR):
            live = ((codes >> code) & 1).astype(F32)
            live_ref[code, tile] = jnp.full((16, TILE), live).astype(BF16)
        observed = jnp.where(count > 0, 1.0, 0.0)
        live_ref[NBR, tile] = jnp.full((16, TILE), observed).astype(BF16)


def clean_kernel(block_count, project_ref, weights_ref, live_ref, *refs):
    block_refs = refs[:block_count]
    cols_ref, near_ref, far_ref, cov_ref = refs[block_count:]
    chan_index = lax.axis_index("chan")
    side = lax.axis_index("patch") % 2
    start = pl.multiple_of(chan_index * REGION, ROW)
    weights = weights_ref[:, pl.ds(start, ROW + REGION + ROW)]
    project = project_ref[...]
    own, masked = [], []
    observed_tiles = jnp.zeros((1, TILE), F32)
    for row in range(EXT):
        lanes = slice(row * ROW, (row + 1) * ROW)
        maps = jnp.concatenate([ref[:, lanes] for ref in block_refs], axis=0)
        split = jnp.concatenate(pieces(maps), axis=0)
        product = jnp.dot(project, split, preferred_element_type=F32)
        cleaned = (product[2 * NCH :] + product[NCH : 2 * NCH]) + product[:NCH]
        weighted = (cleaned * weights[:, lanes]).astype(BF16)
        for col in range(TB):
            tile = weighted[:, col * TILE : (col + 1) * TILE]
            cols_ref[col, row * NCH : (row + 1) * NCH, :] = tile
            if 0 < row <= TA:
                observed = live_ref[NBR, (row - 1) * TB + col]
                observed_tiles = observed_tiles + observed[:1].astype(F32)
                own.append(tile)
                masked.append(tile * jnp.concatenate([observed] * (NCH // 16), axis=0))
    covariance = lax.dot_general(
        jnp.concatenate(masked, axis=1),
        jnp.concatenate(own, axis=1),
        ROWS_BY_ROWS,
        preferred_element_type=F32,
    )
    total = jnp.broadcast_to(observed_tiles[:, :NCH] * float(TILE), (NCH, NCH))
    cov_ref[...] = jnp.concatenate([covariance, total], axis=1)

    rows = lax.broadcasted_iota(jnp.int32, (16, TILE), 0)
    for col in range(TB):
        weight_rows = jnp.zeros((16, TILE), F32)
        for row in range(EXT):
            at = row * ROW + col * TILE
            weight_rows = jnp.where(rows == row, weights[:, at : at + TILE], weight_rows)
        cols_ref[col, WROW:COLH, :] = weight_rows.astype(BF16)
    near_ref[...] = cols_ref[1 - side]
    far_ref[...] = cols_ref[side]


def add_pairs(code, row_shift, live_ref, centres, partners, mask_ref):
    own = slice(NCH, (TA + 1) * NCH)
    left = jnp.concatenate(
        [column[own] for column in centres] + [column[WROW:] for column in centres], axis=0
    )
    binned = jnp.dot(left, mask_ref[code], preferred_element_type=F32).astype(BF16)
    rows = lax.broadcasted_iota(jnp.int32, (16, TILE), 0)
    right = []
    weight_sums = [jnp.zeros((16, TILE), F32) for _ in range(NBIN)]
    for col in range(TB):
        partner_weights = partners[col][WROW:].astype(F32)
        shifted = jnp.zeros((16, TILE), F32)
        for row in range(TA):
            live = live_ref[code, row * TB + col]
            place = row + row_shift
            tile = partners[col][place * NCH : (place + 1) * NCH]
            right.append(tile * jnp.concatenate([live] * (NCH // 16), axis=0))
            weight = partner_weights[place : place + 1] * live.astype(F32)[:1]
            shifted = jnp.where(rows == row + 1, weight, shifted)
        first = TA * TB * NCH + col * 16
        for level in range(NBIN):
            lanes = slice(level * TILE, (level + 1) * TILE)
            weight_sums[level] += binned[first : first + 16, lanes].astype(F32) * shifted
    right = jnp.concatenate(right, axis=1)
    left = jnp.concatenate(
        [
            jnp.concatenate(
                [
                    binned[at * NCH : (at + 1) * NCH, level * TILE : (level + 1) * TILE]
                    for at in range(TA * TB)
                ],
                axis=1,
            )
            for level in range(NBIN)
        ],
        axis=0,
    )
    sums = lax.dot_general(left, right, ROWS_BY_ROWS, preferred_element_type=F32)
    return sums, weight_sums


def pair_kernel(jobs, first, live_ref, mask_ref, cols_ref, *refs):
    halo_refs = {}
    for name in ("near", "far"):
        if any(kind == name for kind, _ in jobs):
            halo_refs[name], *refs = refs
    if not first:
        sums_in_ref, weight_in_ref, *refs = refs
    sums_ref, weight_sums_ref, none_ref = refs
    none_ref[...] = jnp.zeros_like(none_ref)
    even = lax.axis_index("patch") % 2 == 0
    columns = [cols_ref[col] for col in range(TB)]
    for number, (kind, row_shift) in enumerate(jobs):
        if kind == "own":
            code, partners = 3 * row_shift + 1, columns
        else:
            beside = halo_refs[kind][...]
            after = even if kind == "near" else jnp.logical_not(even)
            code = jnp.where(after, 3 * row_shift + 2, 3 * row_shift)
            partners = [
                jnp.where(after, columns[1], beside),
                jnp.where(after, beside, columns[0]),
            ]
        sums, weight_sums = add_pairs(code, row_shift, live_ref, columns, partners, mask_ref)
        if number:
            sums_ref[...] += sums
        else:
            sums_ref[...] = sums if first else sums_in_ref[...] + sums
        for level in range(NBIN):
            if number:
                weight_sums_ref[level] += weight_sums[level]
            elif first:
                weight_sums_ref[level] = weight_sums[level]
            else:
                weight_sums_ref[level] = weight_in_ref[level] + weight_sums[level]


def scale_kernel(sums_ref, weight_sums_ref, *refs):
    *piece_refs, corr_ref, cov_ref = refs
    whole = piece_refs[0][...]
    for ref in piece_refs[1:]:
        whole = whole + ref[...]
    covariance = whole[:, :NCH] / whole[:, NCH:]
    cov_ref[...] = covariance
    channel = lax.broadcasted_iota(jnp.int32, (NCH, NCH), 0)
    other = lax.broadcasted_iota(jnp.int32, (NCH, NCH), 1)
    diagonal = jnp.where(channel == other, covariance, 0.0)
    spread_down = jnp.sqrt(jnp.sum(diagonal, axis=1, keepdims=True) + 1e-06)
    spread_across = jnp.sqrt(jnp.sum(diagonal, axis=0, keepdims=True) + 1e-06)
    norm_scale = spread_down * spread_across
    for level in range(NBIN):
        taper = 0.75 + 0.25 * math.cos(math.pi * level / NBIN)
        total = jnp.sum(
            jnp.sum(weight_sums_ref[level], axis=1, keepdims=True), axis=0, keepdims=True
        )
        pair_weight = jnp.maximum(total, 1.0)
        sums = sums_ref[level * NCH : (level + 1) * NCH]
        corr_ref[level] = (taper * sums) / (pair_weight * norm_scale)


def run(kernel, outs, args, scratch=(), spec=VMEM):
    if spec is HBM:
        args = [pltpu.with_memory_space_constraint(arg, pltpu.HBM) for arg in args]
    return pl.pallas_call(
        kernel,
        out_shape=outs,
        in_specs=[spec] * len(args),
        out_specs=jax.tree.map(lambda _: VMEM, outs),
        scratch_shapes=list(scratch),
        compiler_params=pltpu.CompilerParams(vmem_limit_bytes=24 * 2**20),
    )(*args)


def exchange(x, axis, step):
    count = lax.axis_size(axis)
    return lax.ppermute(x, axis, [(i, i ^ step) for i in range(count)])


def per_device(sky_maps, mode_vectors, pixel_weight, neighbours, tile_counts, pair_bins):
    shape = jax.ShapeDtypeStruct
    chan_count = lax.axis_size("chan")
    patch_count = lax.axis_size("patch")
    local_channels, pixels = sky_maps.shape

    counts = tile_counts.T
    block = shape((local_channels, ROW + REGION + ROW), F32)
    blocks = run(
        prepare_kernel,
        (block,) * chan_count,
        [sky_maps],
        scratch=[pltpu.VMEM((local_channels, pixels), F32), pltpu.SemaphoreType.DMA],
        spec=HBM,
    )
    blocks = [blocks[0]] + [exchange(blocks[s], "chan", s) for s in range(1, chan_count)]
    if local_channels % 16:
        blocks = [jnp.concatenate(blocks, axis=0)]
    project, weights, mask, live = run(
        lambda *refs: setting_kernel(local_channels, *refs),
        (
            shape((3 * NCH, 3 * NCH), BF16),
            shape((1, pixels + 2 * TB * TILE), F32),
            shape((NBR, TILE, NBIN * TILE), BF16),
            shape((NBR + 1, TA * TB, 16, TILE), BF16),
        ),
        [counts, neighbours, mode_vectors.T, pixel_weight.reshape(1, pixels), pair_bins],
        scratch=[
            pltpu.SMEM((TB, TA), jnp.int32),
            pltpu.SMEM((TA, TB, NBR), jnp.int32),
            pltpu.VMEM((MODES, NCH), F32),
            pltpu.VMEM((NBR, TILE, TILE), jnp.int32),
            pltpu.SemaphoreType.DMA((5,)),
        ],
        spec=HBM,
    )

    column = shape((COLH, TILE), BF16)
    piece_shape = shape((NCH, 2 * NCH), F32)
    cols, near, far, piece = run(
        lambda *refs: clean_kernel(len(blocks), *refs),
        (shape((TB, COLH, TILE), BF16), column, column, piece_shape),
        [project, weights, live] + blocks,
    )

    core_piece = exchange(piece, "patch", 1)
    halos = {"near": exchange(near, "patch", 1)}
    far_pairs = [(i, i + 1) for i in range(1, patch_count - 1, 2)]
    halos["far"] = lax.ppermute(far, "patch", far_pairs + [(j, i) for i, j in far_pairs])
    piece = piece + core_piece
    rounds = []
    for axis, stride, count in (("patch", 2, patch_count), ("chan", 1, chan_count)):
        while stride < count:
            group = min(4, count // stride)
            rounds.append((axis, [stride * k for k in range(1, group)]))
            stride *= group
    jobs = [(kind, row_shift) for kind in ("own", "near", "far") for row_shift in range(3)]
    cuts = [jobs[:4], jobs[4:]]
    sums = ()
    for number, (axis, steps) in enumerate(rounds):
        parts = [piece] + [exchange(piece, axis, step) for step in steps]
        none = []
        if number < len(cuts):
            kinds = [kind for kind in halos if any(kind == job[0] for job in cuts[number])]
            *sums, zeros = run(
                lambda *refs: pair_kernel(cuts[number], not number, *refs),
                (shape((NBIN * NCH, NCH), F32), shape((NBIN, 16, TILE), F32), piece_shape),
                [live, mask, cols] + [halos[kind] for kind in kinds] + list(sums),
            )
            none = [zeros]
        if number < len(rounds) - 1:
            piece = sum(parts[1:] + none, parts[0])
    correlation, covariance = run(
        scale_kernel,
        (shape((NBIN, NCH, NCH), F32), shape((NCH, NCH), F32)),
        [*sums, *parts],
    )
    return (correlation[None, None], covariance)


def solution(mesh):
    return jax.shard_map(
        per_device,
        mesh=mesh,
        in_specs=(
            P("chan", "patch"),
            P(),
            P("patch"),
            P("chan", "patch", None),
            P("chan", "patch"),
            P(),
        ),
        out_specs=(P("chan", "patch", None, None, None), P()),
        check_vma=False,
    )
```

```python
import math

import jax
import jax.numpy as jnp
from jax import lax
from jax.experimental import pallas as pl
from jax.experimental.pallas import tpu as pltpu
from jax.sharding import PartitionSpec as P

NCH = 64
MODES = 8
TILE = 128
NBIN = 8
NBR = 9
TA = 3
TB = 2
HALF = NCH // 2
EXT = TA + 2
WROW = EXT * NCH
COLH = WROW + 16
ROW = TB * TILE
SPAN = 2 * TA + 1

F32 = jnp.float32
BF16 = jnp.bfloat16
ROWS_BY_ROWS = (((1,), (1,)), ((), ()))
VMEM = pl.BlockSpec(memory_space=pltpu.VMEM)
HBM = pl.BlockSpec(memory_space=pltpu.HBM)


def pieces(x):
    high = x.astype(BF16)
    rest = x - high.astype(F32)
    middle = rest.astype(BF16)
    low = (rest - middle.astype(F32)).astype(BF16)
    return high, middle, low


def first_row(chan_index):
    return (chan_index - chan_index % 2) * TA - 1 + chan_index % 2


def prepare_kernel(counts_ref, maps_ref, *refs):
    *block_refs, held_counts, held, copied = refs
    chan_index = lax.axis_index("chan")
    local_channels, pixels = maps_ref.shape
    rows = pixels // ROW
    count_copy = pltpu.make_async_copy(counts_ref, held_counts, copied.at[0])
    copy = pltpu.make_async_copy(maps_ref, held, copied.at[1])
    count_copy.start()
    copy.start()
    flag_ref = block_refs[1]
    flag_ref[:, SPAN * ROW :] = jnp.zeros((local_channels, flag_ref.shape[1] - SPAN * ROW), F32)
    count_copy.wait()
    for tile in range(TA * TB):
        observed = jnp.where(held_counts[tile % TB, tile // TB] > 0, 1.0, 0.0)
        row, lane = tile % local_channels, SPAN * ROW + tile // local_channels * TILE
        flag_ref[row : row + 1, lane : lane + TILE] = jnp.full((1, TILE), observed)
    copy.wait()
    for step, ref in enumerate(block_refs):
        first = first_row(chan_index ^ step)
        last = first + SPAN - 1
        above = pl.multiple_of(jnp.maximum(first, 0) * ROW, ROW)
        middle = pl.multiple_of((first + 1) * ROW, ROW)
        below = pl.multiple_of(jnp.minimum(last, rows - 1) * ROW, ROW)
        ref[:, :ROW] = jnp.where(first >= 0, held[:, pl.ds(above, ROW)], 0.0)
        ref[:, ROW : (SPAN - 1) * ROW] = held[:, pl.ds(middle, (SPAN - 2) * ROW)]
        ref[:, (SPAN - 1) * ROW : SPAN * ROW] = jnp.where(
            last < rows, held[:, pl.ds(below, ROW)], 0.0
        )


def setting_kernel(
    local_channels,
    counts_ref,
    neighbours_ref,
    modes_ref,
    weight_ref,
    bins_ref,
    project_ref,
    padded_weight_ref,
    mask_ref,
    live_ref,
    held_counts,
    held_neighbours,
    held_modes,
    held_bins,
    copied,
):
    pixels = weight_ref.shape[1]
    edge = ROW
    pairs = [
        (modes_ref, held_modes),
        (bins_ref, held_bins),
        (weight_ref, padded_weight_ref.at[:, pl.ds(edge, pixels)]),
        (counts_ref, held_counts),
        (neighbours_ref, held_neighbours),
    ]
    copies = [
        pltpu.make_async_copy(source, target, copied.at[number])
        for number, (source, target) in enumerate(pairs)
    ]
    for copy in copies:
        copy.start()
    padded_weight_ref[:, :edge] = jnp.zeros((1, edge), F32)
    padded_weight_ref[:, edge + pixels :] = jnp.zeros((1, edge), F32)
    copies[0].wait()
    vectors = held_modes[...].T
    lane = lax.broadcasted_iota(jnp.int32, (NCH, MODES), 1)
    for number in range(MODES):
        column = jnp.sum(jnp.where(lane == number, vectors, 0.0), axis=1, keepdims=True)
        inner = jnp.sum(column * vectors, axis=0, keepdims=True)
        square = jnp.sum(column * column, axis=0, keepdims=True)
        scale = 1.0 / jnp.sqrt(square + 1e-06)
        unit = column * scale
        reduced = vectors - unit * (inner * scale)
        vectors = jnp.where(lane == number, unit, jnp.where(lane > number, reduced, vectors))
    channel = lax.broadcasted_iota(jnp.int32, (NCH, NCH), 0)
    row = lax.broadcasted_iota(jnp.int32, (NCH, NCH), 1)
    holder = lax.axis_index("chan") ^ (row // local_channels)
    source = holder * local_channels + row % local_channels
    order = jnp.where(channel == source, 1.0, 0.0)
    ordered = lax.dot_general(
        order,
        vectors,
        (((0,), (0,)), ((), ())),
        precision=lax.Precision.HIGHEST,
        preferred_element_type=F32,
    )
    outer = lax.dot_general(
        vectors,
        ordered,
        ROWS_BY_ROWS,
        precision=lax.Precision.HIGHEST,
        preferred_element_type=F32,
    )
    high, middle, low = pieces(order - outer)
    none = jnp.zeros((NCH, NCH), BF16)
    project_ref[0:NCH, :] = jnp.concatenate([high, high, high], axis=1)
    project_ref[NCH : 2 * NCH, :] = jnp.concatenate([middle, middle, none], axis=1)
    project_ref[2 * NCH : 3 * NCH, :] = jnp.concatenate([low, none, none], axis=1)
    copies[1].wait()
    for code in range(NBR):
        table = held_bins[code]
        for level in range(NBIN):
            mask_ref[code, :, level * TILE : (level + 1) * TILE] = jnp.where(
                table == level, 1.0, 0.0
            ).astype(BF16)
    for copy in copies[2:]:
        copy.wait()
    for tile in range(TA * TB):
        count = held_counts[tile % TB, tile // TB]
        codes = jnp.zeros((), jnp.int32)
        for slot in range(NBR):
            code = held_neighbours[tile // TB, tile % TB, slot]
            codes = codes | jnp.where(slot < count, jnp.int32(1) << code, 0)
        for code in range(NBR):
            live = ((codes >> code) & 1).astype(F32)
            live_ref[code, tile] = jnp.full((16, TILE), live).astype(BF16)
        observed = jnp.where(count > 0, 1.0, 0.0)
        live_ref[NBR, tile] = jnp.full((16, TILE), observed).astype(BF16)


def clean_kernel(block_count, project_ref, weights_ref, live_ref, *refs):
    block_refs = refs[:block_count]
    *flag_refs, cols_ref, near_ref, far_ref, cov_ref, tiles_ref = refs[block_count:]
    if flag_refs:
        flags = flag_refs[0][...]
    else:
        flags = block_refs[1][:8, SPAN * ROW :]
    chan_index = lax.axis_index("chan")
    place = chan_index % 2
    side = lax.axis_index("patch") % 2
    start = pl.multiple_of((first_row(chan_index) + 1) * ROW, ROW)
    weights = weights_ref[:, pl.ds(start, SPAN * ROW)]
    project = project_ref[...]
    for row in range(SPAN):
        lanes = slice(row * ROW, (row + 1) * ROW)
        maps = jnp.concatenate([ref[:, lanes] for ref in block_refs], axis=0)
        split = jnp.concatenate(pieces(maps), axis=0)
        product = jnp.dot(project, split, preferred_element_type=F32)
        cleaned = (product[2 * NCH :] + product[NCH : 2 * NCH]) + product[:NCH]
        weighted = (cleaned * weights[:, lanes]).astype(BF16)
        for col in range(TB):
            tiles_ref[row, col] = weighted[:, col * TILE : (col + 1) * TILE]

    both, masked = [], []
    observed_tiles = jnp.zeros((1, TILE), F32)
    for row in range(2 * TA):
        for col in range(TB):
            tile = row % TA * TB + col
            own = live_ref[NBR, tile].astype(F32)[:1]
            observed = jnp.where(place == row // TA, own, flags[tile : tile + 1])
            observed_tiles = observed_tiles + observed
            both.append(tiles_ref[row + 1 - place, col])
            masked.append(both[-1] * jnp.broadcast_to(observed, (NCH, TILE)).astype(BF16))
    both = jnp.concatenate(both, axis=1)
    covariance = lax.dot_general(
        jnp.concatenate(masked, axis=1),
        jnp.concatenate([both, both[HALF:], both[HALF:]], axis=0),
        ROWS_BY_ROWS,
        preferred_element_type=F32,
    )
    lane = lax.broadcasted_iota(jnp.int32, (HALF, TILE), 1)
    lower = jnp.where(lane < 3 * HALF, covariance[HALF:], observed_tiles * float(TILE))
    cov_ref[...] = jnp.where(lane < NCH, covariance[:HALF], lower)

    rows = lax.broadcasted_iota(jnp.int32, (16, TILE), 0)
    for col in range(TB):
        weight_rows = jnp.zeros((16, TILE), F32)
        for row in range(EXT):
            cols_ref[col, row * NCH : (row + 1) * NCH, :] = tiles_ref[2 * place + row, col]
            at = pl.multiple_of((chan_index * TA + row) * ROW + col * TILE, TILE)
            weight_rows = jnp.where(rows == row, weights_ref[:, pl.ds(at, TILE)], weight_rows)
        cols_ref[col, WROW:COLH, :] = weight_rows.astype(BF16)
    near_ref[...] = cols_ref[1 - side]
    far_ref[...] = cols_ref[side]


def add_pairs(code, row_shift, live_ref, centres, partners, mask_ref):
    own = slice(NCH, (TA + 1) * NCH)
    left = jnp.concatenate(
        [column[own] for column in centres] + [column[WROW:] for column in centres], axis=0
    )
    binned = jnp.dot(left, mask_ref[code], preferred_element_type=F32).astype(BF16)
    rows = lax.broadcasted_iota(jnp.int32, (16, TILE), 0)
    right = []
    weight_sums = [jnp.zeros((16, TILE), F32) for _ in range(NBIN)]
    for col in range(TB):
        partner_weights = partners[col][WROW:].astype(F32)
        shifted = jnp.zeros((16, TILE), F32)
        for row in range(TA):
            live = live_ref[code, row * TB + col]
            place = row + row_shift
            tile = partners[col][place * NCH : (place + 1) * NCH]
            right.append(tile * jnp.concatenate([live] * (NCH // 16), axis=0))
            weight = partner_weights[place : place + 1] * live.astype(F32)[:1]
            shifted = jnp.where(rows == row + 1, weight, shifted)
        first = TA * TB * NCH + col * 16
        for level in range(NBIN):
            lanes = slice(level * TILE, (level + 1) * TILE)
            weight_sums[level] += binned[first : first + 16, lanes].astype(F32) * shifted
    right = jnp.concatenate(right, axis=1)
    left = jnp.concatenate(
        [
            jnp.concatenate(
                [
                    binned[at * NCH : (at + 1) * NCH, level * TILE : (level + 1) * TILE]
                    for at in range(TA * TB)
                ],
                axis=1,
            )
            for level in range(NBIN)
        ],
        axis=0,
    )
    sums = lax.dot_general(left, right, ROWS_BY_ROWS, preferred_element_type=F32)
    return sums, weight_sums


def pair_kernel(jobs, first, live_ref, mask_ref, cols_ref, *refs):
    halo_refs = {}
    for name in ("near", "far"):
        if any(kind == name for kind, _ in jobs):
            halo_refs[name], *refs = refs
    if not first:
        sums_in_ref, weight_in_ref, *refs = refs
    sums_ref, weight_sums_ref, none_ref = refs
    none_ref[...] = jnp.zeros_like(none_ref)
    even = lax.axis_index("patch") % 2 == 0
    columns = [cols_ref[col] for col in range(TB)]
    for number, (kind, row_shift) in enumerate(jobs):
        if kind == "own":
            code, partners = 3 * row_shift + 1, columns
        else:
            beside = halo_refs[kind][...]
            after = even if kind == "near" else jnp.logical_not(even)
            code = jnp.where(after, 3 * row_shift + 2, 3 * row_shift)
            partners = [
                jnp.where(after, columns[1], beside),
                jnp.where(after, beside, columns[0]),
            ]
        sums, weight_sums = add_pairs(code, row_shift, live_ref, columns, partners, mask_ref)
        if number:
            sums_ref[...] += sums
        else:
            sums_ref[...] = sums if first else sums_in_ref[...] + sums
        for level in range(NBIN):
            if number:
                weight_sums_ref[level] += weight_sums[level]
            elif first:
                weight_sums_ref[level] = weight_sums[level]
            else:
                weight_sums_ref[level] = weight_in_ref[level] + weight_sums[level]


def scale_kernel(sums_ref, weight_sums_ref, *refs):
    *piece_refs, corr_ref, cov_ref = refs
    whole = piece_refs[0][...]
    for ref in piece_refs[1:]:
        whole = whole + ref[...]
    lane = lax.broadcasted_iota(jnp.int32, (HALF, TILE), 1)
    turned = jnp.concatenate([whole, jnp.zeros((TILE - HALF, TILE), F32)], axis=0).T
    lower = jnp.where(lane < HALF, turned[HALF:NCH], pltpu.roll(whole, TILE - HALF, axis=1))
    covariance = jnp.concatenate([whole, lower], axis=0)[:, :NCH] / whole[:1, TILE - 1 :]
    cov_ref[...] = covariance
    channel = lax.broadcasted_iota(jnp.int32, (NCH, NCH), 0)
    other = lax.broadcasted_iota(jnp.int32, (NCH, NCH), 1)
    diagonal = jnp.where(channel == other, covariance, 0.0)
    spread_down = jnp.sqrt(jnp.sum(diagonal, axis=1, keepdims=True) + 1e-06)
    spread_across = jnp.sqrt(jnp.sum(diagonal, axis=0, keepdims=True) + 1e-06)
    norm_scale = spread_down * spread_across
    for level in range(NBIN):
        taper = 0.75 + 0.25 * math.cos(math.pi * level / NBIN)
        total = jnp.sum(
            jnp.sum(weight_sums_ref[level], axis=1, keepdims=True), axis=0, keepdims=True
        )
        pair_weight = jnp.maximum(total, 1.0)
        sums = sums_ref[level * NCH : (level + 1) * NCH]
        corr_ref[level] = (taper * sums) / (pair_weight * norm_scale)


def run(kernel, outs, args, scratch=(), spec=VMEM):
    if spec is HBM:
        args = [pltpu.with_memory_space_constraint(arg, pltpu.HBM) for arg in args]
    return pl.pallas_call(
        kernel,
        out_shape=outs,
        in_specs=[spec] * len(args),
        out_specs=jax.tree.map(lambda _: VMEM, outs),
        scratch_shapes=list(scratch),
        compiler_params=pltpu.CompilerParams(vmem_limit_bytes=24 * 2**20),
    )(*args)


def exchange(x, axis, step):
    count = lax.axis_size(axis)
    return lax.ppermute(x, axis, [(i, i ^ step) for i in range(count)])


def per_device(sky_maps, mode_vectors, pixel_weight, neighbours, tile_counts, pair_bins):
    shape = jax.ShapeDtypeStruct
    chan_count = lax.axis_size("chan")
    patch_count = lax.axis_size("patch")
    local_channels, pixels = sky_maps.shape

    counts = tile_counts.T
    flag_lanes = -(-TA * TB // local_channels) * TILE
    block_shapes = [
        shape((local_channels, SPAN * ROW + flag_lanes * (step == 1)), F32)
        for step in range(chan_count)
    ]
    blocks = run(
        prepare_kernel,
        tuple(block_shapes),
        [counts, sky_maps],
        scratch=[
            pltpu.SMEM((TB, TA), jnp.int32),
            pltpu.VMEM((local_channels, pixels), F32),
            pltpu.SemaphoreType.DMA((2,)),
        ],
        spec=HBM,
    )
    blocks = [blocks[0]] + [exchange(blocks[s], "chan", s) for s in range(1, chan_count)]
    flags = []
    if local_channels % 16:
        rows = [
            blocks[1][t % local_channels, SPAN * ROW + t // local_channels * TILE :][:TILE]
            for t in range(TA * TB)
        ]
        flags = [jnp.pad(jnp.stack(rows), ((0, 8 - TA * TB), (0, 0)))]
        blocks = [jnp.concatenate([block[:, : SPAN * ROW] for block in blocks], axis=0)]
    project, weights, mask, live = run(
        lambda *refs: setting_kernel(local_channels, *refs),
        (
            shape((3 * NCH, 3 * NCH), BF16),
            shape((1, pixels + 2 * TB * TILE), F32),
            shape((NBR, TILE, NBIN * TILE), BF16),
            shape((NBR + 1, TA * TB, 16, TILE), BF16),
        ),
        [counts, neighbours, mode_vectors.T, pixel_weight.reshape(1, pixels), pair_bins],
        scratch=[
            pltpu.SMEM((TB, TA), jnp.int32),
            pltpu.SMEM((TA, TB, NBR), jnp.int32),
            pltpu.VMEM((MODES, NCH), F32),
            pltpu.VMEM((NBR, TILE, TILE), jnp.int32),
            pltpu.SemaphoreType.DMA((5,)),
        ],
        spec=HBM,
    )

    column = shape((COLH, TILE), BF16)
    piece_shape = shape((HALF, TILE), F32)
    cols, near, far, piece = run(
        lambda *refs: clean_kernel(len(blocks), *refs),
        (shape((TB, COLH, TILE), BF16), column, column, piece_shape),
        [project, weights, live] + blocks + flags,
        scratch=[pltpu.VMEM((SPAN, TB, NCH, TILE), BF16)],
    )

    halos = {"near": exchange(near, "patch", 1)}
    far_pairs = [(i, (i + 1) % patch_count) for i in range(1, patch_count, 2)]
    halos["far"] = lax.ppermute(far, "patch", far_pairs + [(j, i) for i, j in far_pairs])
    rounds = [("patch", [1])]
    for axis, count in (("patch", patch_count), ("chan", chan_count)):
        stride = 2
        while stride < count:
            group = min(4, count // stride)
            rounds.append((axis, [stride * k for k in range(1, group)]))
            stride *= group
    jobs = [(kind, row_shift) for kind in ("own", "near", "far") for row_shift in range(3)]
    cuts = [jobs[:2], jobs[2:6], jobs[6:]]
    sums = ()
    for number, (axis, steps) in enumerate(rounds):
        parts = [piece] + [exchange(piece, axis, step) for step in steps]
        none = []
        if number < len(cuts):
            kinds = [kind for kind in halos if any(kind == job[0] for job in cuts[number])]
            *sums, zeros = run(
                lambda *refs: pair_kernel(cuts[number], not number, *refs),
                (shape((NBIN * NCH, NCH), F32), shape((NBIN, 16, TILE), F32), piece_shape),
                [live, mask, cols] + [halos[kind] for kind in kinds] + list(sums),
            )
            none = [zeros]
        if number < len(rounds) - 1:
            piece = sum(parts[1:] + none, parts[0])
    correlation, covariance = run(
        scale_kernel,
        (shape((NBIN, NCH, NCH), F32), shape((NCH, NCH), F32)),
        [*sums, *parts],
    )
    return (correlation[None, None], covariance)


def solution(mesh):
    return jax.shard_map(
        per_device,
        mesh=mesh,
        in_specs=(
            P("chan", "patch"),
            P(),
            P("patch"),
            P("chan", "patch", None),
            P("chan", "patch"),
            P(),
        ),
        out_specs=(P("chan", "patch", None, None, None), P()),
        check_vma=False,
    )
```

```python
import math

import jax
import jax.numpy as jnp
from jax import lax
from jax.experimental import pallas as pl
from jax.experimental.pallas import tpu as pltpu
from jax.sharding import PartitionSpec as P

NCH = 64
MODES = 8
TILE = 128
NBIN = 8
NBR = 9
TA = 3
TB = 2
HALF = NCH // 2
EXT = TA + 2
WROW = EXT * NCH
COLH = WROW + 16
ROW = TB * TILE
SPAN = 2 * TA + 1

F32 = jnp.float32
BF16 = jnp.bfloat16
ROWS_BY_ROWS = (((1,), (1,)), ((), ()))
VMEM = pl.BlockSpec(memory_space=pltpu.VMEM)
HBM = pl.BlockSpec(memory_space=pltpu.HBM)


def pieces(x):
    high = x.astype(BF16)
    rest = x - high.astype(F32)
    middle = rest.astype(BF16)
    low = (rest - middle.astype(F32)).astype(BF16)
    return high, middle, low


def first_row(chan_index):
    return (chan_index - chan_index % 2) * TA - 1 + chan_index % 2


def prepare_kernel(counts_ref, maps_ref, *refs):
    *block_refs, held_counts, held, copied = refs
    chan_index = lax.axis_index("chan")
    local_channels, pixels = maps_ref.shape
    rows = pixels // ROW
    count_copy = pltpu.make_async_copy(counts_ref, held_counts, copied.at[0])
    copy = pltpu.make_async_copy(maps_ref, held, copied.at[1])
    count_copy.start()
    copy.start()
    flag_ref = block_refs[1]
    flag_ref[:, SPAN * ROW :] = jnp.zeros((local_channels, flag_ref.shape[1] - SPAN * ROW), F32)
    count_copy.wait()
    for tile in range(TA * TB):
        observed = jnp.where(held_counts[tile % TB, tile // TB] > 0, 1.0, 0.0)
        row, lane = tile % local_channels, SPAN * ROW + tile // local_channels * TILE
        flag_ref[row : row + 1, lane : lane + TILE] = jnp.full((1, TILE), observed)
    copy.wait()
    for step, ref in enumerate(block_refs):
        first = first_row(chan_index ^ step)
        last = first + SPAN - 1
        above = pl.multiple_of(jnp.maximum(first, 0) * ROW, ROW)
        middle = pl.multiple_of((first + 1) * ROW, ROW)
        below = pl.multiple_of(jnp.minimum(last, rows - 1) * ROW, ROW)
        ref[:, :ROW] = jnp.where(first >= 0, held[:, pl.ds(above, ROW)], 0.0)
        ref[:, ROW : (SPAN - 1) * ROW] = held[:, pl.ds(middle, (SPAN - 2) * ROW)]
        ref[:, (SPAN - 1) * ROW : SPAN * ROW] = jnp.where(
            last < rows, held[:, pl.ds(below, ROW)], 0.0
        )


def setting_kernel(
    local_channels,
    counts_ref,
    neighbours_ref,
    modes_ref,
    weight_ref,
    bins_ref,
    project_ref,
    padded_weight_ref,
    mask_ref,
    live_ref,
    held_counts,
    held_neighbours,
    held_modes,
    held_bins,
    copied,
):
    pixels = weight_ref.shape[1]
    edge = ROW
    pairs = [
        (modes_ref, held_modes),
        (bins_ref, held_bins),
        (weight_ref, padded_weight_ref.at[:, pl.ds(edge, pixels)]),
        (counts_ref, held_counts),
        (neighbours_ref, held_neighbours),
    ]
    copies = [
        pltpu.make_async_copy(source, target, copied.at[number])
        for number, (source, target) in enumerate(pairs)
    ]
    for copy in copies:
        copy.start()
    padded_weight_ref[:, :edge] = jnp.zeros((1, edge), F32)
    padded_weight_ref[:, edge + pixels :] = jnp.zeros((1, edge), F32)
    copies[0].wait()
    vectors = held_modes[...].T
    lane = lax.broadcasted_iota(jnp.int32, (NCH, MODES), 1)
    for number in range(MODES):
        column = jnp.sum(jnp.where(lane == number, vectors, 0.0), axis=1, keepdims=True)
        inner = jnp.sum(column * vectors, axis=0, keepdims=True)
        square = jnp.sum(column * column, axis=0, keepdims=True)
        scale = 1.0 / jnp.sqrt(square + 1e-06)
        unit = column * scale
        reduced = vectors - unit * (inner * scale)
        vectors = jnp.where(lane == number, unit, jnp.where(lane > number, reduced, vectors))
    channel = lax.broadcasted_iota(jnp.int32, (NCH, NCH), 0)
    row = lax.broadcasted_iota(jnp.int32, (NCH, NCH), 1)
    holder = lax.axis_index("chan") ^ (row // local_channels)
    source = holder * local_channels + row % local_channels
    order = jnp.where(channel == source, 1.0, 0.0)
    ordered = lax.dot_general(
        order,
        vectors,
        (((0,), (0,)), ((), ())),
        precision=lax.Precision.HIGHEST,
        preferred_element_type=F32,
    )
    outer = lax.dot_general(
        vectors,
        ordered,
        ROWS_BY_ROWS,
        precision=lax.Precision.HIGHEST,
        preferred_element_type=F32,
    )
    high, middle, low = pieces(order - outer)
    none = jnp.zeros((NCH, NCH), BF16)
    project_ref[0:NCH, :] = jnp.concatenate([high, high, high], axis=1)
    project_ref[NCH : 2 * NCH, :] = jnp.concatenate([middle, middle, none], axis=1)
    project_ref[2 * NCH : 3 * NCH, :] = jnp.concatenate([low, none, none], axis=1)
    copies[1].wait()
    for code in range(NBR):
        table = held_bins[code]
        for level in range(NBIN):
            mask_ref[code, :, level * TILE : (level + 1) * TILE] = jnp.where(
                table == level, 1.0, 0.0
            ).astype(BF16)
    for copy in copies[2:]:
        copy.wait()
    for tile in range(TA * TB):
        count = held_counts[tile % TB, tile // TB]
        codes = jnp.zeros((), jnp.int32)
        for slot in range(NBR):
            code = held_neighbours[tile // TB, tile % TB, slot]
            codes = codes | jnp.where(slot < count, jnp.int32(1) << code, 0)
        for code in range(NBR):
            live = ((codes >> code) & 1).astype(F32)
            live_ref[code, tile] = jnp.full((16, TILE), live).astype(BF16)
        observed = jnp.where(count > 0, 1.0, 0.0)
        live_ref[NBR, tile] = jnp.full((16, TILE), observed).astype(BF16)


def clean_kernel(block_count, project_ref, weights_ref, live_ref, *refs):
    block_refs = refs[:block_count]
    *flag_refs, cols_ref, near_ref, far_ref, cov_ref, tiles_ref = refs[block_count:]
    if flag_refs:
        flags = flag_refs[0][...]
    else:
        flags = block_refs[1][:8, SPAN * ROW :]
    chan_index = lax.axis_index("chan")
    place = chan_index % 2
    side = lax.axis_index("patch") % 2
    start = pl.multiple_of((first_row(chan_index) + 1) * ROW, ROW)
    weights = weights_ref[:, pl.ds(start, SPAN * ROW)]
    project = project_ref[...]
    for row in range(SPAN):
        lanes = slice(row * ROW, (row + 1) * ROW)
        maps = jnp.concatenate([ref[:, lanes] for ref in block_refs], axis=0)
        split = jnp.concatenate(pieces(maps), axis=0)
        product = jnp.dot(project, split, preferred_element_type=F32)
        cleaned = (product[2 * NCH :] + product[NCH : 2 * NCH]) + product[:NCH]
        weighted = (cleaned * weights[:, lanes]).astype(BF16)
        for col in range(TB):
            tiles_ref[row, col] = weighted[:, col * TILE : (col + 1) * TILE]

    both, masked = [], []
    observed_tiles = jnp.zeros((1, TILE), F32)
    for row in range(2 * TA):
        for col in range(TB):
            tile = row % TA * TB + col
            own = live_ref[NBR, tile].astype(F32)[:1]
            observed = jnp.where(place == row // TA, own, flags[tile : tile + 1])
            observed_tiles = observed_tiles + observed
            both.append(tiles_ref[row + 1 - place, col])
            masked.append(both[-1] * jnp.broadcast_to(observed, (NCH, TILE)).astype(BF16))
    both = jnp.concatenate(both, axis=1)
    covariance = lax.dot_general(
        jnp.concatenate(masked, axis=1),
        jnp.concatenate([both, both[HALF:], both[HALF:]], axis=0),
        ROWS_BY_ROWS,
        preferred_element_type=F32,
    )
    lane = lax.broadcasted_iota(jnp.int32, (HALF, TILE), 1)
    lower = jnp.where(lane < 3 * HALF, covariance[HALF:], observed_tiles * float(TILE))
    cov_ref[...] = jnp.where(lane < NCH, covariance[:HALF], lower)

    rows = lax.broadcasted_iota(jnp.int32, (16, TILE), 0)
    for col in range(TB):
        weight_rows = jnp.zeros((16, TILE), F32)
        for row in range(EXT):
            cols_ref[col, row * NCH : (row + 1) * NCH, :] = tiles_ref[2 * place + row, col]
            at = pl.multiple_of((chan_index * TA + row) * ROW + col * TILE, TILE)
            weight_rows = jnp.where(rows == row, weights_ref[:, pl.ds(at, TILE)], weight_rows)
        cols_ref[col, WROW:COLH, :] = weight_rows.astype(BF16)
    near_ref[...] = cols_ref[1 - side]
    far_ref[...] = cols_ref[side]


def add_pairs(code, row_shift, live_ref, centres, partners, mask_ref):
    own = slice(NCH, (TA + 1) * NCH)
    left = jnp.concatenate(
        [column[own] for column in centres] + [column[WROW:] for column in centres], axis=0
    )
    binned = jnp.dot(left, mask_ref[code], preferred_element_type=F32).astype(BF16)
    rows = lax.broadcasted_iota(jnp.int32, (16, TILE), 0)
    right = []
    weight_sums = [jnp.zeros((16, TILE), F32) for _ in range(NBIN)]
    for col in range(TB):
        partner_weights = partners[col][WROW:].astype(F32)
        shifted = jnp.zeros((16, TILE), F32)
        for row in range(TA):
            live = live_ref[code, row * TB + col]
            place = row + row_shift
            tile = partners[col][place * NCH : (place + 1) * NCH]
            right.append(tile * jnp.concatenate([live] * (NCH // 16), axis=0))
            weight = partner_weights[place : place + 1] * live.astype(F32)[:1]
            shifted = jnp.where(rows == row + 1, weight, shifted)
        first = TA * TB * NCH + col * 16
        for level in range(NBIN):
            lanes = slice(level * TILE, (level + 1) * TILE)
            weight_sums[level] += binned[first : first + 16, lanes].astype(F32) * shifted
    right = jnp.concatenate(right, axis=1)
    left = jnp.concatenate(
        [
            jnp.concatenate(
                [
                    binned[at * NCH : (at + 1) * NCH, level * TILE : (level + 1) * TILE]
                    for at in range(TA * TB)
                ],
                axis=1,
            )
            for level in range(NBIN)
        ],
        axis=0,
    )
    sums = lax.dot_general(left, right, ROWS_BY_ROWS, preferred_element_type=F32)
    return sums, weight_sums


def pair_kernel(jobs, first, live_ref, mask_ref, cols_ref, *refs):
    halo_refs = {}
    for name in ("near", "far"):
        if any(kind == name for kind, _ in jobs):
            halo_refs[name], *refs = refs
    if not first:
        sums_in_ref, weight_in_ref, *refs = refs
    sums_ref, weight_sums_ref, *none_refs = refs
    for ref in none_refs:
        ref[...] = jnp.zeros_like(ref)
    even = lax.axis_index("patch") % 2 == 0
    columns = [cols_ref[col] for col in range(TB)]
    after = {"near": even, "far": jnp.logical_not(even)}
    partners = {"own": columns}
    for kind, ref in halo_refs.items():
        partners[kind] = [
            jnp.where(after[kind], columns[1], ref[...]),
            jnp.where(after[kind], ref[...], columns[0]),
        ]
    for number, (kind, row_shift) in enumerate(jobs):
        code = 3 * row_shift + 1
        if kind != "own":
            code = code + jnp.where(after[kind], 1, -1)
        sums, weight_sums = add_pairs(
            code, row_shift, live_ref, columns, partners[kind], mask_ref
        )
        if number:
            sums_ref[...] += sums
        else:
            sums_ref[...] = sums if first else sums_in_ref[...] + sums
        for level in range(NBIN):
            if number:
                weight_sums_ref[level] += weight_sums[level]
            elif first:
                weight_sums_ref[level] = weight_sums[level]
            else:
                weight_sums_ref[level] = weight_in_ref[level] + weight_sums[level]


def scale_kernel(sums_ref, weight_sums_ref, *refs):
    *piece_refs, corr_ref, cov_ref = refs
    whole = piece_refs[0][...]
    for ref in piece_refs[1:]:
        whole = whole + ref[...]
    lane = lax.broadcasted_iota(jnp.int32, (HALF, TILE), 1)
    turned = jnp.concatenate([whole, jnp.zeros((TILE - HALF, TILE), F32)], axis=0).T
    lower = jnp.where(lane < HALF, turned[HALF:NCH], pltpu.roll(whole, TILE - HALF, axis=1))
    covariance = jnp.concatenate([whole, lower], axis=0)[:, :NCH] / whole[:1, TILE - 1 :]
    cov_ref[...] = covariance
    channel = lax.broadcasted_iota(jnp.int32, (NCH, NCH), 0)
    other = lax.broadcasted_iota(jnp.int32, (NCH, NCH), 1)
    diagonal = jnp.where(channel == other, covariance, 0.0)
    spread_down = jnp.sqrt(jnp.sum(diagonal, axis=1, keepdims=True) + 1e-06)
    spread_across = jnp.sqrt(jnp.sum(diagonal, axis=0, keepdims=True) + 1e-06)
    norm_scale = spread_down * spread_across
    for level in range(NBIN):
        taper = 0.75 + 0.25 * math.cos(math.pi * level / NBIN)
        total = jnp.sum(
            jnp.sum(weight_sums_ref[level], axis=1, keepdims=True), axis=0, keepdims=True
        )
        pair_weight = jnp.maximum(total, 1.0)
        sums = sums_ref[level * NCH : (level + 1) * NCH]
        corr_ref[level] = (taper * sums) / (pair_weight * norm_scale)


def run(kernel, outs, args, scratch=(), spec=VMEM):
    if spec is HBM:
        args = [pltpu.with_memory_space_constraint(arg, pltpu.HBM) for arg in args]
    return pl.pallas_call(
        kernel,
        out_shape=outs,
        in_specs=[spec] * len(args),
        out_specs=jax.tree.map(lambda _: VMEM, outs),
        scratch_shapes=list(scratch),
        compiler_params=pltpu.CompilerParams(vmem_limit_bytes=24 * 2**20),
    )(*args)


def exchange(x, axis, step):
    count = lax.axis_size(axis)
    return lax.ppermute(x, axis, [(i, i ^ step) for i in range(count)])


def per_device(sky_maps, mode_vectors, pixel_weight, neighbours, tile_counts, pair_bins):
    shape = jax.ShapeDtypeStruct
    chan_count = lax.axis_size("chan")
    patch_count = lax.axis_size("patch")
    local_channels, pixels = sky_maps.shape

    counts = tile_counts.T
    flag_lanes = -(-TA * TB // local_channels) * TILE
    block_shapes = [
        shape((local_channels, SPAN * ROW + flag_lanes * (step == 1)), F32)
        for step in range(chan_count)
    ]
    blocks = run(
        prepare_kernel,
        tuple(block_shapes),
        [counts, sky_maps],
        scratch=[
            pltpu.SMEM((TB, TA), jnp.int32),
            pltpu.VMEM((local_channels, pixels), F32),
            pltpu.SemaphoreType.DMA((2,)),
        ],
        spec=HBM,
    )
    blocks = [blocks[0]] + [exchange(blocks[s], "chan", s) for s in range(1, chan_count)]
    flags = []
    if local_channels % 16:
        rows = [
            blocks[1][t % local_channels, SPAN * ROW + t // local_channels * TILE :][:TILE]
            for t in range(TA * TB)
        ]
        flags = [jnp.pad(jnp.stack(rows), ((0, 8 - TA * TB), (0, 0)))]
        blocks = [jnp.concatenate([block[:, : SPAN * ROW] for block in blocks], axis=0)]
    project, weights, mask, live = run(
        lambda *refs: setting_kernel(local_channels, *refs),
        (
            shape((3 * NCH, 3 * NCH), BF16),
            shape((1, pixels + 2 * TB * TILE), F32),
            shape((NBR, TILE, NBIN * TILE), BF16),
            shape((NBR + 1, TA * TB, 16, TILE), BF16),
        ),
        [counts, neighbours, mode_vectors.T, pixel_weight.reshape(1, pixels), pair_bins],
        scratch=[
            pltpu.SMEM((TB, TA), jnp.int32),
            pltpu.SMEM((TA, TB, NBR), jnp.int32),
            pltpu.VMEM((MODES, NCH), F32),
            pltpu.VMEM((NBR, TILE, TILE), jnp.int32),
            pltpu.SemaphoreType.DMA((5,)),
        ],
        spec=HBM,
    )

    column = shape((COLH, TILE), BF16)
    piece_shape = shape((HALF, TILE), F32)
    cols, near, far, piece = run(
        lambda *refs: clean_kernel(len(blocks), *refs),
        (shape((TB, COLH, TILE), BF16), column, column, piece_shape),
        [project, weights, live] + blocks + flags,
        scratch=[pltpu.VMEM((SPAN, TB, NCH, TILE), BF16)],
    )

    halos = {"near": exchange(near, "patch", 1)}
    far_pairs = [(i, (i + 1) % patch_count) for i in range(1, patch_count, 2)]
    halos["far"] = lax.ppermute(far, "patch", far_pairs + [(j, i) for i, j in far_pairs])
    rounds = [("patch", [1])]
    for axis, count in (("patch", patch_count), ("chan", chan_count)):
        stride = 2
        while stride < count:
            group = min(4, count // stride)
            rounds.append((axis, [stride * k for k in range(1, group)]))
            stride *= group
    jobs = [(kind, row_shift) for kind in ("own", "near", "far") for row_shift in range(3)]
    cuts = [jobs[:1], jobs[1:5], jobs[5:]]
    sums = ()
    for number, (axis, steps) in enumerate(rounds):
        parts = [piece] + [exchange(piece, axis, step) for step in steps]
        none = []
        if number < len(cuts):
            kinds = [kind for kind in halos if any(kind == job[0] for job in cuts[number])]
            last = number == len(rounds) - 1
            outs = (shape((NBIN * NCH, NCH), F32), shape((NBIN, 16, TILE), F32))
            outs = run(
                lambda *refs: pair_kernel(cuts[number], not number, *refs),
                outs if last else outs + (piece_shape,),
                [live, mask, cols] + [halos[kind] for kind in kinds] + list(sums),
            )
            sums, none = outs[:2], list(outs[2:])
        if number < len(rounds) - 1:
            piece = sum(parts[1:] + none, parts[0])
    correlation, covariance = run(
        scale_kernel,
        (shape((NBIN, NCH, NCH), F32), shape((NCH, NCH), F32)),
        [*sums, *parts],
    )
    return (correlation[None, None], covariance)


def solution(mesh):
    return jax.shard_map(
        per_device,
        mesh=mesh,
        in_specs=(
            P("chan", "patch"),
            P(),
            P("patch"),
            P("chan", "patch", None),
            P("chan", "patch"),
            P(),
        ),
        out_specs=(P("chan", "patch", None, None, None), P()),
        check_vma=False,
    )
```

```python
import math

import jax
import jax.numpy as jnp
from jax import lax
from jax.experimental import pallas as pl
from jax.experimental.pallas import tpu as pltpu
from jax.sharding import PartitionSpec as P

NCH = 64
MODES = 8
TILE = 128
NBIN = 8
NBR = 9
TA = 3
TB = 2
HALF = NCH // 2
EXT = TA + 2
WROW = EXT * NCH
COLH = WROW + 16
ROW = TB * TILE
SPAN = 2 * TA + 1

F32 = jnp.float32
BF16 = jnp.bfloat16
ROWS_BY_ROWS = (((1,), (1,)), ((), ()))
VMEM = pl.BlockSpec(memory_space=pltpu.VMEM)
HBM = pl.BlockSpec(memory_space=pltpu.HBM)


def pieces(x):
    high = x.astype(BF16)
    rest = x - high.astype(F32)
    middle = rest.astype(BF16)
    low = (rest - middle.astype(F32)).astype(BF16)
    return high, middle, low


def first_row(chan_index):
    return (chan_index - chan_index % 2) * TA - 1 + chan_index % 2


def prepare_kernel(counts_ref, maps_ref, *refs):
    *block_refs, held_counts, held, copied = refs
    chan_index = lax.axis_index("chan")
    local_channels, pixels = maps_ref.shape
    rows = pixels // ROW
    count_copy = pltpu.make_async_copy(counts_ref, held_counts, copied.at[0])
    copy = pltpu.make_async_copy(maps_ref, held, copied.at[1])
    count_copy.start()
    copy.start()
    flag_ref = block_refs[1]
    flag_ref[:, SPAN * ROW :] = jnp.zeros((local_channels, flag_ref.shape[1] - SPAN * ROW), F32)
    count_copy.wait()
    for tile in range(TA * TB):
        observed = jnp.where(held_counts[tile % TB, tile // TB] > 0, 1.0, 0.0)
        row, lane = tile % local_channels, SPAN * ROW + tile // local_channels * TILE
        flag_ref[row : row + 1, lane : lane + TILE] = jnp.full((1, TILE), observed)
    copy.wait()
    for step, ref in enumerate(block_refs):
        first = first_row(chan_index ^ step)
        last = first + SPAN - 1
        above = pl.multiple_of(jnp.maximum(first, 0) * ROW, ROW)
        middle = pl.multiple_of((first + 1) * ROW, ROW)
        below = pl.multiple_of(jnp.minimum(last, rows - 1) * ROW, ROW)
        ref[:, :ROW] = jnp.where(first >= 0, held[:, pl.ds(above, ROW)], 0.0)
        ref[:, ROW : (SPAN - 1) * ROW] = held[:, pl.ds(middle, (SPAN - 2) * ROW)]
        ref[:, (SPAN - 1) * ROW : SPAN * ROW] = jnp.where(
            last < rows, held[:, pl.ds(below, ROW)], 0.0
        )


def setting_kernel(
    local_channels,
    counts_ref,
    neighbours_ref,
    modes_ref,
    weight_ref,
    bins_ref,
    project_ref,
    padded_weight_ref,
    mask_ref,
    live_ref,
    held_counts,
    held_neighbours,
    held_modes,
    held_bins,
    copied,
):
    pixels = weight_ref.shape[1]
    edge = ROW
    pairs = [
        (modes_ref, held_modes),
        (bins_ref, held_bins),
        (weight_ref, padded_weight_ref.at[:, pl.ds(edge, pixels)]),
        (counts_ref, held_counts),
        (neighbours_ref, held_neighbours),
    ]
    copies = [
        pltpu.make_async_copy(source, target, copied.at[number])
        for number, (source, target) in enumerate(pairs)
    ]
    for copy in copies:
        copy.start()
    padded_weight_ref[:, :edge] = jnp.zeros((1, edge), F32)
    padded_weight_ref[:, edge + pixels :] = jnp.zeros((1, edge), F32)
    copies[0].wait()
    vectors = held_modes[...].T
    lane = lax.broadcasted_iota(jnp.int32, (NCH, MODES), 1)
    for number in range(MODES):
        column = jnp.sum(jnp.where(lane == number, vectors, 0.0), axis=1, keepdims=True)
        inner = jnp.sum(column * vectors, axis=0, keepdims=True)
        square = jnp.sum(column * column, axis=0, keepdims=True)
        scale = 1.0 / jnp.sqrt(square + 1e-06)
        unit = column * scale
        reduced = vectors - unit * (inner * scale)
        vectors = jnp.where(lane == number, unit, jnp.where(lane > number, reduced, vectors))
    channel = lax.broadcasted_iota(jnp.int32, (NCH, NCH), 0)
    row = lax.broadcasted_iota(jnp.int32, (NCH, NCH), 1)
    holder = lax.axis_index("chan") ^ (row // local_channels)
    source = holder * local_channels + row % local_channels
    order = jnp.where(channel == source, 1.0, 0.0)
    ordered = lax.dot_general(
        order,
        vectors,
        (((0,), (0,)), ((), ())),
        precision=lax.Precision.HIGHEST,
        preferred_element_type=F32,
    )
    outer = lax.dot_general(
        vectors,
        ordered,
        ROWS_BY_ROWS,
        precision=lax.Precision.HIGHEST,
        preferred_element_type=F32,
    )
    high, middle, low = pieces(order - outer)
    none = jnp.zeros((NCH, NCH), BF16)
    project_ref[0:NCH, :] = jnp.concatenate([high, high, high], axis=1)
    project_ref[NCH : 2 * NCH, :] = jnp.concatenate([middle, middle, none], axis=1)
    project_ref[2 * NCH : 3 * NCH, :] = jnp.concatenate([low, none, none], axis=1)
    copies[1].wait()
    for code in range(NBR):
        table = held_bins[code]
        for level in range(NBIN):
            mask_ref[code, :, level * TILE : (level + 1) * TILE] = jnp.where(
                table == level, 1.0, 0.0
            ).astype(BF16)
    for copy in copies[2:]:
        copy.wait()
    for tile in range(TA * TB):
        count = held_counts[tile % TB, tile // TB]
        codes = jnp.zeros((), jnp.int32)
        for slot in range(NBR):
            code = held_neighbours[tile // TB, tile % TB, slot]
            codes = codes | jnp.where(slot < count, jnp.int32(1) << code, 0)
        for code in range(NBR):
            live = ((codes >> code) & 1).astype(F32)
            live_ref[code, tile] = jnp.full((16, TILE), live).astype(BF16)
        observed = jnp.where(count > 0, 1.0, 0.0)
        live_ref[NBR, tile] = jnp.full((16, TILE), observed).astype(BF16)


def clean_kernel(block_count, project_ref, weights_ref, live_ref, *refs):
    block_refs = refs[:block_count]
    *flag_refs, cols_ref, near_ref, far_ref, cov_ref, tiles_ref = refs[block_count:]
    if flag_refs:
        flags = flag_refs[0][...]
    else:
        flags = block_refs[1][:8, SPAN * ROW :]
    chan_index = lax.axis_index("chan")
    place = chan_index % 2
    side = lax.axis_index("patch") % 2
    start = pl.multiple_of((first_row(chan_index) + 1) * ROW, ROW)
    weights = weights_ref[:, pl.ds(start, SPAN * ROW)]
    project = project_ref[...]
    for row in range(SPAN):
        lanes = slice(row * ROW, (row + 1) * ROW)
        maps = jnp.concatenate([ref[:, lanes] for ref in block_refs], axis=0)
        split = jnp.concatenate(pieces(maps), axis=0)
        product = jnp.dot(project, split, preferred_element_type=F32)
        cleaned = (product[2 * NCH :] + product[NCH : 2 * NCH]) + product[:NCH]
        weighted = (cleaned * weights[:, lanes]).astype(BF16)
        for col in range(TB):
            tiles_ref[row, col] = weighted[:, col * TILE : (col + 1) * TILE]

    both, masked = [], []
    observed_tiles = jnp.zeros((1, TILE), F32)
    for row in range(2 * TA):
        for col in range(TB):
            tile = row % TA * TB + col
            own = live_ref[NBR, tile].astype(F32)[:1]
            observed = jnp.where(place == row // TA, own, flags[tile : tile + 1])
            observed_tiles = observed_tiles + observed
            both.append(tiles_ref[row + 1 - place, col])
            masked.append(both[-1] * jnp.broadcast_to(observed, (NCH, TILE)).astype(BF16))
    both = jnp.concatenate(both, axis=1)
    covariance = lax.dot_general(
        jnp.concatenate(masked, axis=1),
        jnp.concatenate([both, both[HALF:], both[HALF:]], axis=0),
        ROWS_BY_ROWS,
        preferred_element_type=F32,
    )
    lane = lax.broadcasted_iota(jnp.int32, (HALF, TILE), 1)
    lower = jnp.where(lane < 3 * HALF, covariance[HALF:], observed_tiles * float(TILE))
    cov_ref[...] = jnp.where(lane < NCH, covariance[:HALF], lower)

    rows = lax.broadcasted_iota(jnp.int32, (16, TILE), 0)
    for col in range(TB):
        weight_rows = jnp.zeros((16, TILE), F32)
        for row in range(EXT):
            cols_ref[col, row * NCH : (row + 1) * NCH, :] = tiles_ref[2 * place + row, col]
            at = pl.multiple_of((chan_index * TA + row) * ROW + col * TILE, TILE)
            weight_rows = jnp.where(rows == row, weights_ref[:, pl.ds(at, TILE)], weight_rows)
        cols_ref[col, WROW:COLH, :] = weight_rows.astype(BF16)
    near_ref[...] = cols_ref[1 - side]
    far_ref[...] = cols_ref[side]


def add_pairs(code, row_shift, live_ref, centres, partners, mask_ref):
    own = slice(NCH, (TA + 1) * NCH)
    left = jnp.concatenate(
        [column[own] for column in centres] + [column[WROW:] for column in centres], axis=0
    )
    binned = jnp.dot(left, mask_ref[code], preferred_element_type=F32).astype(BF16)
    rows = lax.broadcasted_iota(jnp.int32, (16, TILE), 0)
    right = []
    weight_sums = [jnp.zeros((16, TILE), F32) for _ in range(NBIN)]
    for col in range(TB):
        partner_weights = partners[col][WROW:].astype(F32)
        shifted = jnp.zeros((16, TILE), F32)
        for row in range(TA):
            live = live_ref[code, row * TB + col]
            place = row + row_shift
            tile = partners[col][place * NCH : (place + 1) * NCH]
            right.append(tile * jnp.concatenate([live] * (NCH // 16), axis=0))
            weight = partner_weights[place : place + 1] * live.astype(F32)[:1]
            shifted = jnp.where(rows == row + 1, weight, shifted)
        first = TA * TB * NCH + col * 16
        for level in range(NBIN):
            lanes = slice(level * TILE, (level + 1) * TILE)
            weight_sums[level] += binned[first : first + 16, lanes].astype(F32) * shifted
    right = jnp.concatenate(right, axis=1)
    left = jnp.concatenate(
        [
            jnp.concatenate(
                [
                    binned[at * NCH : (at + 1) * NCH, level * TILE : (level + 1) * TILE]
                    for at in range(TA * TB)
                ],
                axis=1,
            )
            for level in range(NBIN)
        ],
        axis=0,
    )
    sums = lax.dot_general(left, right, ROWS_BY_ROWS, preferred_element_type=F32)
    return sums, weight_sums


def pair_kernel(jobs, first, live_ref, mask_ref, cols_ref, *refs):
    halo_refs = {}
    for name in ("near", "far"):
        if any(kind == name for kind, _ in jobs):
            halo_refs[name], *refs = refs
    if not first:
        sums_in_ref, weight_in_ref, *refs = refs
    sums_ref, weight_sums_ref, *none_refs = refs
    for ref in none_refs:
        ref[...] = jnp.zeros_like(ref)
    even = lax.axis_index("patch") % 2 == 0
    columns = [cols_ref[col] for col in range(TB)]
    after = {"near": even, "far": jnp.logical_not(even)}
    partners = {"own": columns}
    for kind, ref in halo_refs.items():
        partners[kind] = [
            jnp.where(after[kind], columns[1], ref[...]),
            jnp.where(after[kind], ref[...], columns[0]),
        ]
    for number, (kind, row_shift) in enumerate(jobs):
        code = 3 * row_shift + 1
        if kind != "own":
            code = code + jnp.where(after[kind], 1, -1)
        sums, weight_sums = add_pairs(
            code, row_shift, live_ref, columns, partners[kind], mask_ref
        )
        if number:
            sums_ref[...] += sums
        else:
            sums_ref[...] = sums if first else sums_in_ref[...] + sums
        for level in range(NBIN):
            if number:
                weight_sums_ref[level] += weight_sums[level]
            elif first:
                weight_sums_ref[level] = weight_sums[level]
            else:
                weight_sums_ref[level] = weight_in_ref[level] + weight_sums[level]


def scale_kernel(sums_ref, weight_sums_ref, *refs):
    *piece_refs, corr_ref, cov_ref = refs
    whole = piece_refs[0][...]
    for ref in piece_refs[1:]:
        whole = whole + ref[...]
    lane = lax.broadcasted_iota(jnp.int32, (HALF, TILE), 1)
    turned = jnp.concatenate([whole, jnp.zeros((TILE - HALF, TILE), F32)], axis=0).T
    lower = jnp.where(lane < HALF, turned[HALF:NCH], pltpu.roll(whole, TILE - HALF, axis=1))
    covariance = jnp.concatenate([whole, lower], axis=0)[:, :NCH] / whole[:1, TILE - 1 :]
    cov_ref[...] = covariance
    channel = lax.broadcasted_iota(jnp.int32, (NCH, NCH), 0)
    other = lax.broadcasted_iota(jnp.int32, (NCH, NCH), 1)
    diagonal = jnp.where(channel == other, covariance, 0.0)
    spread_down = jnp.sqrt(jnp.sum(diagonal, axis=1, keepdims=True) + 1e-06)
    spread_across = jnp.sqrt(jnp.sum(diagonal, axis=0, keepdims=True) + 1e-06)
    norm_scale = spread_down * spread_across
    for level in range(NBIN):
        taper = 0.75 + 0.25 * math.cos(math.pi * level / NBIN)
        total = jnp.sum(
            jnp.sum(weight_sums_ref[level], axis=1, keepdims=True), axis=0, keepdims=True
        )
        pair_weight = jnp.maximum(total, 1.0)
        sums = sums_ref[level * NCH : (level + 1) * NCH]
        corr_ref[level] = (taper * sums) / (pair_weight * norm_scale)


def run(kernel, outs, args, scratch=(), spec=VMEM):
    if spec is HBM:
        args = [pltpu.with_memory_space_constraint(arg, pltpu.HBM) for arg in args]
    return pl.pallas_call(
        kernel,
        out_shape=outs,
        in_specs=[spec] * len(args),
        out_specs=jax.tree.map(lambda _: VMEM, outs),
        scratch_shapes=list(scratch),
        compiler_params=pltpu.CompilerParams(vmem_limit_bytes=24 * 2**20),
    )(*args)


def exchange(x, axis, step):
    count = lax.axis_size(axis)
    return lax.ppermute(x, axis, [(i, i ^ step) for i in range(count)])


def exchange_across(x, chan_step, patch_step):
    if not chan_step:
        return exchange(x, "patch", patch_step)
    if not patch_step:
        return exchange(x, "chan", chan_step)
    count = lax.axis_size("patch")
    pairs = [
        (chan * count + patch, (chan ^ chan_step) * count + (patch ^ patch_step))
        for chan in range(lax.axis_size("chan"))
        for patch in range(count)
    ]
    return lax.ppermute(x, ("chan", "patch"), pairs)


def sum_rounds(chan_count, patch_count):
    far = [(0, 1 << n) for n in range(2, patch_count.bit_length() - 1)]
    far += [(1 << n, 0) for n in range(2, chan_count.bit_length() - 1)]
    groups = [[(0, 1)]] + [far[at : at + 2] for at in range(0, len(far), 2)] + [[(0, 2), (2, 0)]]
    rounds = []
    for group in groups:
        partners = [(0, 0)]
        for chan_step, patch_step in group:
            partners += [(chan ^ chan_step, patch ^ patch_step) for chan, patch in partners]
        rounds.append(partners[1:])
    return rounds


def per_device(sky_maps, mode_vectors, pixel_weight, neighbours, tile_counts, pair_bins):
    shape = jax.ShapeDtypeStruct
    chan_count = lax.axis_size("chan")
    patch_count = lax.axis_size("patch")
    local_channels, pixels = sky_maps.shape

    counts = tile_counts.T
    flag_lanes = -(-TA * TB // local_channels) * TILE
    block_shapes = [
        shape((local_channels, SPAN * ROW + flag_lanes * (step == 1)), F32)
        for step in range(chan_count)
    ]
    blocks = run(
        prepare_kernel,
        tuple(block_shapes),
        [counts, sky_maps],
        scratch=[
            pltpu.SMEM((TB, TA), jnp.int32),
            pltpu.VMEM((local_channels, pixels), F32),
            pltpu.SemaphoreType.DMA((2,)),
        ],
        spec=HBM,
    )
    blocks = [blocks[0]] + [exchange(blocks[s], "chan", s) for s in range(1, chan_count)]
    flags = []
    if local_channels % 16:
        rows = [
            blocks[1][t % local_channels, SPAN * ROW + t // local_channels * TILE :][:TILE]
            for t in range(TA * TB)
        ]
        flags = [jnp.pad(jnp.stack(rows), ((0, 8 - TA * TB), (0, 0)))]
        blocks = [jnp.concatenate([block[:, : SPAN * ROW] for block in blocks], axis=0)]
    project, weights, mask, live = run(
        lambda *refs: setting_kernel(local_channels, *refs),
        (
            shape((3 * NCH, 3 * NCH), BF16),
            shape((1, pixels + 2 * TB * TILE), F32),
            shape((NBR, TILE, NBIN * TILE), BF16),
            shape((NBR + 1, TA * TB, 16, TILE), BF16),
        ),
        [counts, neighbours, mode_vectors.T, pixel_weight.reshape(1, pixels), pair_bins],
        scratch=[
            pltpu.SMEM((TB, TA), jnp.int32),
            pltpu.SMEM((TA, TB, NBR), jnp.int32),
            pltpu.VMEM((MODES, NCH), F32),
            pltpu.VMEM((NBR, TILE, TILE), jnp.int32),
            pltpu.SemaphoreType.DMA((5,)),
        ],
        spec=HBM,
    )

    column = shape((COLH, TILE), BF16)
    piece_shape = shape((HALF, TILE), F32)
    cols, near, far, piece = run(
        lambda *refs: clean_kernel(len(blocks), *refs),
        (shape((TB, COLH, TILE), BF16), column, column, piece_shape),
        [project, weights, live] + blocks + flags,
        scratch=[pltpu.VMEM((SPAN, TB, NCH, TILE), BF16)],
    )

    halos = {"near": exchange(near, "patch", 1)}
    far_pairs = [(i, (i + 1) % patch_count) for i in range(1, patch_count, 2)]
    halos["far"] = lax.ppermute(far, "patch", far_pairs + [(j, i) for i, j in far_pairs])
    rounds = sum_rounds(chan_count, patch_count)
    jobs = [(kind, row_shift) for kind in ("own", "near", "far") for row_shift in range(3)]
    cuts = [jobs[:1], jobs[1:5], jobs[5:]]
    sums = ()
    for number, partners in enumerate(rounds):
        parts = [piece] + [exchange_across(piece, *steps) for steps in partners]
        none = []
        if number < len(cuts):
            kinds = [kind for kind in halos if any(kind == job[0] for job in cuts[number])]
            last = number == len(rounds) - 1
            outs = (shape((NBIN * NCH, NCH), F32), shape((NBIN, 16, TILE), F32))
            outs = run(
                lambda *refs: pair_kernel(cuts[number], not number, *refs),
                outs if last else outs + (piece_shape,),
                [live, mask, cols] + [halos[kind] for kind in kinds] + list(sums),
            )
            sums, none = outs[:2], list(outs[2:])
        if number < len(rounds) - 1:
            piece = sum(parts[1:] + none, parts[0])
    correlation, covariance = run(
        scale_kernel,
        (shape((NBIN, NCH, NCH), F32), shape((NCH, NCH), F32)),
        [*sums, *parts],
    )
    return (correlation[None, None], covariance)


def solution(mesh):
    return jax.shard_map(
        per_device,
        mesh=mesh,
        in_specs=(
            P("chan", "patch"),
            P(),
            P("patch"),
            P("chan", "patch", None),
            P("chan", "patch"),
            P(),
        ),
        out_specs=(P("chan", "patch", None, None, None), P()),
        check_vma=False,
    )
```

```python
import math

import jax
import jax.numpy as jnp
from jax import lax
from jax.experimental import pallas as pl
from jax.experimental.pallas import tpu as pltpu
from jax.sharding import PartitionSpec as P

NCH = 64
MODES = 8
TILE = 128
NBIN = 8
NBR = 9
TA = 3
TB = 2
HALF = NCH // 2
EXT = TA + 2
WROW = EXT * NCH
COLH = WROW + 16
ROW = TB * TILE
SPAN = 2 * TA + 1

F32 = jnp.float32
BF16 = jnp.bfloat16
ROWS_BY_ROWS = (((1,), (1,)), ((), ()))
VMEM = pl.BlockSpec(memory_space=pltpu.VMEM)
HBM = pl.BlockSpec(memory_space=pltpu.HBM)


def pieces(x):
    high = x.astype(BF16)
    rest = x - high.astype(F32)
    middle = rest.astype(BF16)
    low = (rest - middle.astype(F32)).astype(BF16)
    return high, middle, low


def first_row(chan_index):
    return (chan_index - chan_index % 2) * TA - 1 + chan_index % 2


def prepare_kernel(counts_ref, maps_ref, *refs):
    *block_refs, held_counts, held, copied = refs
    chan_index = lax.axis_index("chan")
    local_channels, pixels = maps_ref.shape
    rows = pixels // ROW
    count_copy = pltpu.make_async_copy(counts_ref, held_counts, copied.at[0])
    copy = pltpu.make_async_copy(maps_ref, held, copied.at[1])
    count_copy.start()
    copy.start()
    flag_ref = block_refs[1]
    flag_ref[:, SPAN * ROW :] = jnp.zeros((local_channels, flag_ref.shape[1] - SPAN * ROW), F32)
    count_copy.wait()
    for tile in range(TA * TB):
        observed = jnp.where(held_counts[tile % TB, tile // TB] > 0, 1.0, 0.0)
        row, lane = tile % local_channels, SPAN * ROW + tile // local_channels * TILE
        flag_ref[row : row + 1, lane : lane + TILE] = jnp.full((1, TILE), observed)
    copy.wait()
    for step, ref in enumerate(block_refs):
        first = first_row(chan_index ^ step)
        last = first + SPAN - 1
        above = pl.multiple_of(jnp.maximum(first, 0) * ROW, ROW)
        middle = pl.multiple_of((first + 1) * ROW, ROW)
        below = pl.multiple_of(jnp.minimum(last, rows - 1) * ROW, ROW)
        ref[:, :ROW] = jnp.where(first >= 0, held[:, pl.ds(above, ROW)], 0.0)
        ref[:, ROW : (SPAN - 1) * ROW] = held[:, pl.ds(middle, (SPAN - 2) * ROW)]
        ref[:, (SPAN - 1) * ROW : SPAN * ROW] = jnp.where(
            last < rows, held[:, pl.ds(below, ROW)], 0.0
        )


def setting_kernel(
    local_channels,
    counts_ref,
    neighbours_ref,
    modes_ref,
    weight_ref,
    bins_ref,
    project_ref,
    padded_weight_ref,
    mask_ref,
    live_ref,
    held_counts,
    held_neighbours,
    held_modes,
    held_bins,
    copied,
):
    pixels = weight_ref.shape[1]
    edge = ROW
    pairs = [
        (modes_ref, held_modes),
        (bins_ref, held_bins),
        (weight_ref, padded_weight_ref.at[:, pl.ds(edge, pixels)]),
        (counts_ref, held_counts),
        (neighbours_ref, held_neighbours),
    ]
    copies = [
        pltpu.make_async_copy(source, target, copied.at[number])
        for number, (source, target) in enumerate(pairs)
    ]
    for copy in copies:
        copy.start()
    padded_weight_ref[:, :edge] = jnp.zeros((1, edge), F32)
    padded_weight_ref[:, edge + pixels :] = jnp.zeros((1, edge), F32)
    copies[0].wait()
    vectors = held_modes[...].T
    lane = lax.broadcasted_iota(jnp.int32, (NCH, MODES), 1)
    for number in range(MODES):
        column = jnp.sum(jnp.where(lane == number, vectors, 0.0), axis=1, keepdims=True)
        inner = jnp.sum(column * vectors, axis=0, keepdims=True)
        square = jnp.sum(column * column, axis=0, keepdims=True)
        scale = 1.0 / jnp.sqrt(square + 1e-06)
        unit = column * scale
        reduced = vectors - unit * (inner * scale)
        vectors = jnp.where(lane == number, unit, jnp.where(lane > number, reduced, vectors))
    channel = lax.broadcasted_iota(jnp.int32, (NCH, NCH), 0)
    row = lax.broadcasted_iota(jnp.int32, (NCH, NCH), 1)
    holder = lax.axis_index("chan") ^ (row // local_channels)
    source = holder * local_channels + row % local_channels
    order = jnp.where(channel == source, 1.0, 0.0)
    ordered = lax.dot_general(
        order,
        vectors,
        (((0,), (0,)), ((), ())),
        precision=lax.Precision.HIGHEST,
        preferred_element_type=F32,
    )
    outer = lax.dot_general(
        vectors,
        ordered,
        ROWS_BY_ROWS,
        precision=lax.Precision.HIGHEST,
        preferred_element_type=F32,
    )
    high, middle, low = pieces(order - outer)
    none = jnp.zeros((NCH, NCH), BF16)
    project_ref[0:NCH, :] = jnp.concatenate([high, high, high], axis=1)
    project_ref[NCH : 2 * NCH, :] = jnp.concatenate([middle, middle, none], axis=1)
    project_ref[2 * NCH : 3 * NCH, :] = jnp.concatenate([low, none, none], axis=1)
    copies[1].wait()
    for code in range(NBR):
        table = held_bins[code]
        for level in range(NBIN):
            mask_ref[code, :, level * TILE : (level + 1) * TILE] = jnp.where(
                table == level, 1.0, 0.0
            ).astype(BF16)
    for copy in copies[2:]:
        copy.wait()
    for tile in range(TA * TB):
        count = held_counts[tile % TB, tile // TB]
        codes = jnp.zeros((), jnp.int32)
        for slot in range(NBR):
            code = held_neighbours[tile // TB, tile % TB, slot]
            codes = codes | jnp.where(slot < count, jnp.int32(1) << code, 0)
        for code in range(NBR):
            live = ((codes >> code) & 1).astype(F32)
            live_ref[code, tile] = jnp.full((16, TILE), live).astype(BF16)
        observed = jnp.where(count > 0, 1.0, 0.0)
        live_ref[NBR, tile] = jnp.full((16, TILE), observed).astype(BF16)


def clean_kernel(block_count, project_ref, weights_ref, live_ref, *refs):
    block_refs = refs[:block_count]
    *flag_refs, cols_ref, near_ref, far_ref, cov_ref, tiles_ref = refs[block_count:]
    if flag_refs:
        flags = flag_refs[0][...]
    else:
        flags = block_refs[1][:8, SPAN * ROW :]
    chan_index = lax.axis_index("chan")
    place = chan_index % 2
    side = lax.axis_index("patch") % 2
    start = pl.multiple_of((first_row(chan_index) + 1) * ROW, ROW)
    weights = weights_ref[:, pl.ds(start, SPAN * ROW)]
    project = project_ref[...]
    for row in range(SPAN):
        lanes = slice(row * ROW, (row + 1) * ROW)
        maps = jnp.concatenate([ref[:, lanes] for ref in block_refs], axis=0)
        split = jnp.concatenate(pieces(maps), axis=0)
        product = jnp.dot(project, split, preferred_element_type=F32)
        cleaned = (product[2 * NCH :] + product[NCH : 2 * NCH]) + product[:NCH]
        weighted = (cleaned * weights[:, lanes]).astype(BF16)
        for col in range(TB):
            tiles_ref[row, col] = weighted[:, col * TILE : (col + 1) * TILE]

    both, masked = [], []
    observed_tiles = jnp.zeros((1, TILE), F32)
    for row in range(2 * TA):
        for col in range(TB):
            tile = row % TA * TB + col
            own = live_ref[NBR, tile].astype(F32)[:1]
            observed = jnp.where(place == row // TA, own, flags[tile : tile + 1])
            observed_tiles = observed_tiles + observed
            both.append(tiles_ref[row + 1 - place, col])
            masked.append(both[-1] * jnp.broadcast_to(observed, (NCH, TILE)).astype(BF16))
    both = jnp.concatenate(both, axis=1)
    covariance = lax.dot_general(
        jnp.concatenate(masked, axis=1),
        jnp.concatenate([both, both[HALF:], both[HALF:]], axis=0),
        ROWS_BY_ROWS,
        preferred_element_type=F32,
    )
    lane = lax.broadcasted_iota(jnp.int32, (HALF, TILE), 1)
    lower = jnp.where(lane < 3 * HALF, covariance[HALF:], observed_tiles * float(TILE))
    cov_ref[...] = jnp.where(lane < NCH, covariance[:HALF], lower)

    rows = lax.broadcasted_iota(jnp.int32, (16, TILE), 0)
    for col in range(TB):
        weight_rows = jnp.zeros((16, TILE), F32)
        for row in range(EXT):
            cols_ref[col, row * NCH : (row + 1) * NCH, :] = tiles_ref[2 * place + row, col]
            at = pl.multiple_of((chan_index * TA + row) * ROW + col * TILE, TILE)
            weight_rows = jnp.where(rows == row, weights_ref[:, pl.ds(at, TILE)], weight_rows)
        cols_ref[col, WROW:COLH, :] = weight_rows.astype(BF16)
    near_ref[...] = cols_ref[1 - side]
    far_ref[...] = cols_ref[side]


def add_pairs(code, row_shift, live_ref, centres, partners, mask_ref):
    own = slice(NCH, (TA + 1) * NCH)
    left = jnp.concatenate(
        [column[own] for column in centres] + [column[WROW:] for column in centres], axis=0
    )
    binned = jnp.dot(left, mask_ref[code], preferred_element_type=F32).astype(BF16)
    rows = lax.broadcasted_iota(jnp.int32, (16, TILE), 0)
    right = []
    weight_sums = [jnp.zeros((16, TILE), F32) for _ in range(NBIN)]
    for col in range(TB):
        partner_weights = partners[col][WROW:].astype(F32)
        shifted = jnp.zeros((16, TILE), F32)
        for row in range(TA):
            live = live_ref[code, row * TB + col]
            place = row + row_shift
            tile = partners[col][place * NCH : (place + 1) * NCH]
            right.append(tile * jnp.concatenate([live] * (NCH // 16), axis=0))
            weight = partner_weights[place : place + 1] * live.astype(F32)[:1]
            shifted = jnp.where(rows == row + 1, weight, shifted)
        first = TA * TB * NCH + col * 16
        for level in range(NBIN):
            lanes = slice(level * TILE, (level + 1) * TILE)
            weight_sums[level] += binned[first : first + 16, lanes].astype(F32) * shifted
    right = jnp.concatenate(right, axis=1)
    left = jnp.concatenate(
        [
            jnp.concatenate(
                [
                    binned[at * NCH : (at + 1) * NCH, level * TILE : (level + 1) * TILE]
                    for at in range(TA * TB)
                ],
                axis=1,
            )
            for level in range(NBIN)
        ],
        axis=0,
    )
    sums = lax.dot_general(left, right, ROWS_BY_ROWS, preferred_element_type=F32)
    return sums, weight_sums


def pair_kernel(jobs, first, live_ref, mask_ref, cols_ref, *refs):
    halo_refs = {}
    for name in ("near", "far"):
        if any(kind == name for kind, _ in jobs):
            halo_refs[name], *refs = refs
    if not first:
        sums_in_ref, weight_in_ref, *refs = refs
    sums_ref, weight_sums_ref, *none_refs = refs
    for ref in none_refs:
        ref[...] = jnp.zeros_like(ref)
    even = lax.axis_index("patch") % 2 == 0
    columns = [cols_ref[col] for col in range(TB)]
    after = {"near": even, "far": jnp.logical_not(even)}
    partners = {"own": columns}
    for kind, ref in halo_refs.items():
        partners[kind] = [
            jnp.where(after[kind], columns[1], ref[...]),
            jnp.where(after[kind], ref[...], columns[0]),
        ]
    for number, (kind, row_shift) in enumerate(jobs):
        code = 3 * row_shift + 1
        if kind != "own":
            code = code + jnp.where(after[kind], 1, -1)
        sums, weight_sums = add_pairs(
            code, row_shift, live_ref, columns, partners[kind], mask_ref
        )
        if number:
            sums_ref[...] += sums
        else:
            sums_ref[...] = sums if first else sums_in_ref[...] + sums
        for level in range(NBIN):
            if number:
                weight_sums_ref[level] += weight_sums[level]
            elif first:
                weight_sums_ref[level] = weight_sums[level]
            else:
                weight_sums_ref[level] = weight_in_ref[level] + weight_sums[level]


def scale_kernel(sums_ref, weight_sums_ref, *refs):
    *piece_refs, corr_ref, cov_ref = refs
    whole = piece_refs[0][...]
    for ref in piece_refs[1:]:
        whole = whole + ref[...]
    lane = lax.broadcasted_iota(jnp.int32, (HALF, TILE), 1)
    turned = jnp.concatenate([whole, jnp.zeros((TILE - HALF, TILE), F32)], axis=0).T
    lower = jnp.where(lane < HALF, turned[HALF:NCH], pltpu.roll(whole, TILE - HALF, axis=1))
    covariance = jnp.concatenate([whole, lower], axis=0)[:, :NCH] / whole[:1, TILE - 1 :]
    cov_ref[...] = covariance
    channel = lax.broadcasted_iota(jnp.int32, (NCH, NCH), 0)
    other = lax.broadcasted_iota(jnp.int32, (NCH, NCH), 1)
    diagonal = jnp.where(channel == other, covariance, 0.0)
    spread_down = jnp.sqrt(jnp.sum(diagonal, axis=1, keepdims=True) + 1e-06)
    spread_across = jnp.sqrt(jnp.sum(diagonal, axis=0, keepdims=True) + 1e-06)
    norm_scale = spread_down * spread_across
    for level in range(NBIN):
        taper = 0.75 + 0.25 * math.cos(math.pi * level / NBIN)
        total = jnp.sum(
            jnp.sum(weight_sums_ref[level], axis=1, keepdims=True), axis=0, keepdims=True
        )
        pair_weight = jnp.maximum(total, 1.0)
        sums = sums_ref[level * NCH : (level + 1) * NCH]
        corr_ref[level] = (taper * sums) / (pair_weight * norm_scale)


def run(kernel, outs, args, scratch=(), spec=VMEM):
    if spec is HBM:
        args = [pltpu.with_memory_space_constraint(arg, pltpu.HBM) for arg in args]
    return pl.pallas_call(
        kernel,
        out_shape=outs,
        in_specs=[spec] * len(args),
        out_specs=jax.tree.map(lambda _: VMEM, outs),
        scratch_shapes=list(scratch),
        compiler_params=pltpu.CompilerParams(vmem_limit_bytes=24 * 2**20),
    )(*args)


def exchange(x, axis, step):
    count = lax.axis_size(axis)
    return lax.ppermute(x, axis, [(i, i ^ step) for i in range(count)])


def exchange_across(x, chan_step, patch_step):
    if not chan_step:
        return exchange(x, "patch", patch_step)
    if not patch_step:
        return exchange(x, "chan", chan_step)
    count = lax.axis_size("patch")
    pairs = [
        (chan * count + patch, (chan ^ chan_step) * count + (patch ^ patch_step))
        for chan in range(lax.axis_size("chan"))
        for patch in range(count)
    ]
    return lax.ppermute(x, ("chan", "patch"), pairs)


def sum_rounds(chan_count, patch_count):
    far = [(0, 1 << n) for n in range(2, patch_count.bit_length() - 1)]
    far += [(1 << n, 0) for n in range(2, chan_count.bit_length() - 1)]
    groups = [[(0, 1)]] + [far[at : at + 2] for at in range(0, len(far), 2)] + [[(0, 2), (2, 0)]]
    rounds = []
    for group in groups:
        partners = [(0, 0)]
        for chan_step, patch_step in group:
            partners += [(chan ^ chan_step, patch ^ patch_step) for chan, patch in partners]
        rounds.append([(chan, patch | 1) for chan, patch in partners[1:]])
    return rounds


def per_device(sky_maps, mode_vectors, pixel_weight, neighbours, tile_counts, pair_bins):
    shape = jax.ShapeDtypeStruct
    chan_count = lax.axis_size("chan")
    patch_count = lax.axis_size("patch")
    local_channels, pixels = sky_maps.shape

    counts = tile_counts.T
    flag_lanes = -(-TA * TB // local_channels) * TILE
    block_shapes = [
        shape((local_channels, SPAN * ROW + flag_lanes * (step == 1)), F32)
        for step in range(chan_count)
    ]
    blocks = run(
        prepare_kernel,
        tuple(block_shapes),
        [counts, sky_maps],
        scratch=[
            pltpu.SMEM((TB, TA), jnp.int32),
            pltpu.VMEM((local_channels, pixels), F32),
            pltpu.SemaphoreType.DMA((2,)),
        ],
        spec=HBM,
    )
    blocks = [blocks[0]] + [exchange(blocks[s], "chan", s) for s in range(1, chan_count)]
    flags = []
    if local_channels % 16:
        rows = [
            blocks[1][t % local_channels, SPAN * ROW + t // local_channels * TILE :][:TILE]
            for t in range(TA * TB)
        ]
        flags = [jnp.pad(jnp.stack(rows), ((0, 8 - TA * TB), (0, 0)))]
        blocks = [jnp.concatenate([block[:, : SPAN * ROW] for block in blocks], axis=0)]
    project, weights, mask, live = run(
        lambda *refs: setting_kernel(local_channels, *refs),
        (
            shape((3 * NCH, 3 * NCH), BF16),
            shape((1, pixels + 2 * TB * TILE), F32),
            shape((NBR, TILE, NBIN * TILE), BF16),
            shape((NBR + 1, TA * TB, 16, TILE), BF16),
        ),
        [counts, neighbours, mode_vectors.T, pixel_weight.reshape(1, pixels), pair_bins],
        scratch=[
            pltpu.SMEM((TB, TA), jnp.int32),
            pltpu.SMEM((TA, TB, NBR), jnp.int32),
            pltpu.VMEM((MODES, NCH), F32),
            pltpu.VMEM((NBR, TILE, TILE), jnp.int32),
            pltpu.SemaphoreType.DMA((5,)),
        ],
        spec=HBM,
    )

    column = shape((COLH, TILE), BF16)
    piece_shape = shape((HALF, TILE), F32)
    cols, near, far, piece = run(
        lambda *refs: clean_kernel(len(blocks), *refs),
        (shape((TB, COLH, TILE), BF16), column, column, piece_shape),
        [project, weights, live] + blocks + flags,
        scratch=[pltpu.VMEM((SPAN, TB, NCH, TILE), BF16)],
    )

    halos = {"near": exchange(near, "patch", 1)}
    far_pairs = [(i, (i + 1) % patch_count) for i in range(1, patch_count, 2)]
    halos["far"] = lax.ppermute(far, "patch", far_pairs + [(j, i) for i, j in far_pairs])
    rounds = sum_rounds(chan_count, patch_count)
    jobs = [(kind, row_shift) for kind in ("own", "near", "far") for row_shift in range(3)]
    cuts = [jobs[:1], jobs[1:5], jobs[5:]]
    sums = ()
    for number, partners in enumerate(rounds):
        parts = [piece] + [exchange_across(piece, *steps) for steps in partners]
        none = []
        if number < len(cuts):
            kinds = [kind for kind in halos if any(kind == job[0] for job in cuts[number])]
            last = number == len(rounds) - 1
            outs = (shape((NBIN * NCH, NCH), F32), shape((NBIN, 16, TILE), F32))
            outs = run(
                lambda *refs: pair_kernel(cuts[number], not number, *refs),
                outs if last else outs + (piece_shape,),
                [live, mask, cols] + [halos[kind] for kind in kinds] + list(sums),
            )
            sums, none = outs[:2], list(outs[2:])
        if number < len(rounds) - 1:
            piece = sum(parts[1:] + none, parts[0])
    correlation, covariance = run(
        scale_kernel,
        (shape((NBIN, NCH, NCH), F32), shape((NCH, NCH), F32)),
        [*sums, *parts],
    )
    return (correlation[None, None], covariance)


def solution(mesh):
    return jax.shard_map(
        per_device,
        mesh=mesh,
        in_specs=(
            P("chan", "patch"),
            P(),
            P("patch"),
            P("chan", "patch", None),
            P("chan", "patch"),
            P(),
        ),
        out_specs=(P("chan", "patch", None, None, None), P()),
        check_vma=False,
    )
```
